256 devices in a mesh: section: 8 (over z_lo, core), expert: 16 (over y, x), dp: 2 (over z_hi).
Axes of the slice: x: 4, y: 4, z: 8 (z_hi: 2, z_lo: 4; z = z_hi * 4 + z_lo), core: 2. Of those that a mesh axis runs over, the one named last changes fastest.
Arguments:
- fwd_input: bfloat16 [8, 4096, 3584], P('section', ('expert', 'dp')), may hold values from -6 to 6
- fwd_routes: int32 [8, 4096, 1], P('section', ('expert', 'dp')), may hold values from 0 to 7; in each aligned block of 128 rows (0 to 127, 128 to 255, ..., all dimensions but the last counted through in order) at most 24 rows name the same one
- fwd_gates: int32 [8, 4096, 1], P('section', ('expert', 'dp')), may hold values from 1 to 65535
- bwd_input: bfloat16 [8, 4096, 3584], P('section', ('expert', 'dp')), may hold values from -6 to 6
- bwd_cotangent: bfloat16 [8, 4096, 3584], P('section', ('expert', 'dp')), may hold values from -6 to 6
- bwd_routes: int32 [8, 4096, 1], P('section', ('expert', 'dp')), may hold values from 0 to 7; in each aligned block of 128 rows (0 to 127, 128 to 255, ..., all dimensions but the last counted through in order) at most 24 rows name the same one
- bwd_gates: int32 [8, 4096, 1], P('section', ('expert', 'dp')), may hold values from 1 to 65535
- norm_gain: float32 [8, 3584], P('section'), may hold values from 0.5 to 1.5
- w_gate: bfloat16 [8, 16, 3584, 512], P('section', 'expert', 'dp'), may hold values from -0.09375 to 0.09375
- w_up: bfloat16 [8, 16, 3584, 512], P('section', 'expert', 'dp'), may hold values from -0.09375 to 0.09375
- w_down: bfloat16 [8, 16, 512, 3584], P('section', 'expert', 'dp'), may hold values from -0.1875 to 0.1875
Outputs:
- fwd_next: bfloat16 [8, 4096, 3584], P('section', ('expert', 'dp'))
- bwd_next: bfloat16 [8, 4096, 3584], P('section', ('expert', 'dp'))
- gain_grad: float32 [8, 3584], P('section')
The draws below stay inside these ranges and needn't reach their ends.
Inputs may be any that keep to these rules, and one draw needn't show every extreme that they name: `fwd_routes`: each token names 1 different experts; among the 128 rows of one device no expert is named more than 24 times, a bound that some block reaches. `bwd_routes`: each token names 1 different experts; among the 128 rows of one device no expert is named more than 24 times, a bound that some block reaches.
All inputs are finite; a program needn't handle non-finite values.
Results may differ from the reference program's by a relative error of at most 0.0073.
Values may be sent and summed in bfloat16 or wider, within the bound.
A program may use at most 128 MiB of HBM per device.

```python
import math
import jax
import jax.numpy as jnp
import numpy as np
from jax import lax

D = 3584
FE = 1024
TOPK = 1
TOK_DEV = 128
EXPERTS = 8
CAP = 24
TOKENS = 4096
N_SECTION = 8
N_EXPERT = 16
N_DP = 2


def touch_ends(values, stream_key, smallest, largest):
    longest = values.shape.index(max(values.shape))
    spots = []
    for shift in (0, 1):
        where = [jax.random.randint(jax.random.fold_in(stream_key, axis), (), 0, length) for axis, length in enumerate(values.shape)]
        where[longest] = (where[longest] + shift) % values.shape[longest]
        spots.append(tuple(where))
    return values.at[spots[0]].set(smallest).at[spots[1]].set(largest)


def level_of(rng, extent, split, smallest, high):
    loudness = 1.0
    for position, blocks in split:
        steps = jax.random.uniform(jax.random.fold_in(jax.random.fold_in(rng, 6), position), (blocks,), jnp.float32, smallest / len(split), high / len(split))
        loudness = loudness * jnp.repeat(jnp.exp(steps), extent[position] // blocks).reshape((-1,) + (1,) * (len(extent) - 1 - position))
    return loudness


def deal_out(key, own, number, rows, amount, top, limit, lean):
    order = jax.random.permutation(key, amount)
    heavy_load, ordinary = portions_of(amount, rows * top, limit, lean, True), portions_of(amount, rows * top, limit, lean, False)
    places = jnp.arange(amount)

    def named(sizes, rotation):
        used = int((sizes > 0).sum())
        fixed = max(1, used // 4)
        shifted = fixed + (places - fixed + rotation * (used - fixed)) % max(1, amount - fixed)
        return jnp.zeros((amount,), jnp.int32).at[order[jnp.where(places < fixed, places, shifted)]].set(jnp.asarray(sizes, jnp.int32))

    sizes = jnp.where(number % 4 == 0, named(heavy_load, number // 4), named(ordinary, number - number // 4 - 1))
    mixed = jax.random.permutation(jax.random.fold_in(own, 3), amount)
    source_of, sink = mixed[0:amount // 2 * 2:2], mixed[1:amount // 2 * 2:2]
    margin = jnp.minimum(sizes[source_of] - 1, limit - sizes[sink]) // 2
    margin = jnp.where((source_of == order[0]) | (sink == order[0]) | (sizes[sink] == 0), 0, jnp.maximum(margin, 0))
    shifted = jax.random.randint(jax.random.fold_in(own, 4), (amount // 2,), 0, 1 << 20) % (margin + 1)
    sizes = sizes.at[source_of].add(-shifted).at[sink].add(shifted)
    members = jnp.searchsorted(jnp.cumsum(sizes), jnp.arange(rows * top), side="right").astype(jnp.int32)
    table = members.reshape(top, rows).T
    table = table[jax.random.permutation(jax.random.fold_in(own, 1), rows)]
    rotation = jax.random.randint(jax.random.fold_in(own, 2), (rows, 1), 0, top)
    return jnp.take_along_axis(table, (jnp.arange(top)[None, :] + rotation) % top, axis=1)


def portions_of(count, total, bound, skew, full):
    weights = [(1 << 20) // math.isqrt(standing ** skew) + 1 for standing in range(1, count + 1)]
    largest = bound if full else min(bound, max(-(-total // count), total * weights[0] // sum(weights)))
    least = 1 if total - largest >= count - 1 else 0
    holding, surplus = [largest] + [least] * (count - 1), total - largest - least * (count - 1)
    while surplus > 0:
        movable = [i for i in range(1, count) if holding[i] < largest] or [i for i in range(1, count) if holding[i] < bound]
        mass, remaining = sum([weights[i] for i in movable]), surplus
        for i in movable:
            addition = min(bound - holding[i], max(1, remaining * weights[i] // mass), surplus)
            holding[i] = holding[i] + addition
            surplus = surplus - addition
    return np.array(holding)


def bell_draw(rng, dims, scale, most, cuts=(), kind=jnp.bfloat16):
    result = jax.random.normal(rng, dims, jnp.float32) * scale
    if len(cuts) > 0:
        result = level_of(rng, dims, cuts, -0.22, 0.18) * result
    return jnp.clip(result, min=-most, max=most).astype(kind)


def setup_inputs(seed: int = 0) -> dict:
    splits = jax.random.split(jax.random.key(seed), 12)
    fwd_input = bell_draw(splits[0], (N_SECTION, TOKENS, D), 1.0, 6.0, ((0, 8), (1, 32)))
    fwd_routes_keys = jax.random.split(jax.random.fold_in(splits[1], 1), N_SECTION * TOKENS // TOK_DEV)
    fwd_routes_turns = jax.random.permutation(jax.random.fold_in(splits[1], 3), N_SECTION * TOKENS // TOK_DEV)
    fwd_routes = jax.vmap(lambda own, number: deal_out(jax.random.fold_in(splits[1], 2), own, number, TOK_DEV, EXPERTS, TOPK, CAP, 2))(fwd_routes_keys, fwd_routes_turns).reshape((N_SECTION, TOKENS, TOPK))
    fwd_gates = touch_ends(jax.random.randint(splits[2], (N_SECTION, TOKENS, TOPK), 1, 65536), jax.random.fold_in(splits[2], 1), 1, 65535).astype(jnp.int32)
    bwd_input = bell_draw(splits[3], (N_SECTION, TOKENS, D), 1.0, 6.0, ((0, 8), (1, 32)))
    bwd_cotangent = bell_draw(splits[4], (N_SECTION, TOKENS, D), 1.0, 6.0, ((0, 8), (1, 32)))
    bwd_routes_keys = jax.random.split(jax.random.fold_in(splits[5], 1), N_SECTION * TOKENS // TOK_DEV)
    bwd_routes_turns = jax.random.permutation(jax.random.fold_in(splits[5], 3), N_SECTION * TOKENS // TOK_DEV)
    bwd_routes = jax.vmap(lambda own, number: deal_out(jax.random.fold_in(splits[5], 2), own, number, TOK_DEV, EXPERTS, TOPK, CAP, 2))(bwd_routes_keys, bwd_routes_turns).reshape((N_SECTION, TOKENS, TOPK))
    bwd_gates = touch_ends(jax.random.randint(splits[6], (N_SECTION, TOKENS, TOPK), 1, 65536), jax.random.fold_in(splits[6], 1), 1, 65535).astype(jnp.int32)
    norm_gain = jnp.clip(1.0 + 0.1 * jax.random.normal(splits[7], (N_SECTION, D), jnp.float32), 0.5, 1.5)
    w_gate = bell_draw(splits[8], (N_SECTION, 2 * EXPERTS, D, FE // 2), D ** -0.5, 0.09375, ((0, 8), (1, 16), (2, 2)))
    w_up = bell_draw(splits[9], (N_SECTION, 2 * EXPERTS, D, FE // 2), D ** -0.5, 0.09375, ((0, 8), (1, 16), (2, 2)))
    w_down = bell_draw(splits[10], (N_SECTION, 2 * EXPERTS, FE // 2, D), FE ** -0.5, 0.1875, ((0, 8), (1, 16), (2, 2)))
    return dict(fwd_input=fwd_input, fwd_routes=fwd_routes, fwd_gates=fwd_gates, bwd_input=bwd_input, bwd_cotangent=bwd_cotangent, bwd_routes=bwd_routes, bwd_gates=bwd_gates, norm_gain=norm_gain, w_gate=w_gate, w_up=w_up, w_down=w_down)


eps = 1e-06
fixed_scale = 65536.0

def rounded(values):
    return lax.optimization_barrier(values.astype(jnp.bfloat16)).astype(jnp.float32)

def slot_positions(route_block):
    flat_ids = route_block.reshape(-1).astype(jnp.int32)
    onehot = (flat_ids[:, None] == jnp.arange(EXPERTS, dtype=jnp.int32)[None, :]).astype(jnp.int32)
    earlier = jnp.cumsum(onehot, axis=0) - onehot
    order_rank = lax.optimization_barrier(jnp.sum(earlier * onehot, axis=1))
    return (flat_ids * CAP + order_rank).astype(jnp.int32)

def place_rows(row_data, slot_index):
    filled = jnp.zeros((EXPERTS * CAP, D), row_data.dtype).at[slot_index].set(row_data)
    return filled.reshape(EXPERTS, CAP, D)

def normalize(inputs, gain_row):
    values = inputs.astype(jnp.float32)
    inverse = lax.rsqrt(lax.optimization_barrier(jnp.mean(values * values, axis=-1, keepdims=True)) + eps)
    return (values, inverse, (values * inverse * gain_row).astype(jnp.bfloat16))

def to_experts(hidden_rows, slots):
    buffers = jax.vmap(place_rows)(hidden_rows, slots)
    blocks = buffers.shape[0]
    return buffers.transpose(1, 0, 2, 3).reshape(EXPERTS, blocks * CAP, D)

def from_experts(expert_rows, slots):
    blocks = slots.shape[0]
    back = expert_rows.reshape(EXPERTS, blocks, CAP, D).transpose(1, 0, 2, 3).reshape(blocks, EXPERTS * CAP, D)
    picked = jax.vmap(lambda block_rows, index: block_rows[index])(back, slots)
    return picked.reshape(blocks, TOK_DEV, TOPK, D).astype(jnp.float32)

def reference(fwd_input, fwd_routes, fwd_gates, bwd_input, bwd_cotangent, bwd_routes, bwd_gates, norm_gain, w_gate, w_up, w_down):
    blocks = N_EXPERT * N_DP
    half_width = FE // 2
    outs_fwd, outs_bwd, gains = ([], [], [])
    for section_index in range(N_SECTION):
        gain_row = norm_gain[section_index]
        gate_halves = w_gate[section_index].astype(jnp.float32).reshape(EXPERTS, 2, D, half_width)
        up_halves = w_up[section_index].astype(jnp.float32).reshape(EXPERTS, 2, D, half_width)
        down_halves = w_down[section_index].astype(jnp.float32).reshape(EXPERTS, 2, half_width, D)
        values, inverse, normed = normalize(fwd_input[section_index].reshape(blocks, TOK_DEV, D), gain_row)
        slots = jax.vmap(slot_positions)(fwd_routes[section_index].reshape(blocks, TOK_DEV, TOPK))
        weights = fwd_gates[section_index].reshape(blocks, TOK_DEV, TOPK).astype(jnp.float32) / fixed_scale
        rows_in = to_experts(jnp.repeat(normed, TOPK, axis=1), slots).astype(jnp.float32)
        half_outs = []
        for half in range(2):
            gate_act = jnp.einsum('erd,edf->erf', rows_in, gate_halves[:, half])
            up_act = jnp.einsum('erd,edf->erf', rows_in, up_halves[:, half])
            hidden_act = rounded(jax.nn.silu(gate_act) * up_act)
            half_outs.append(rounded(jnp.einsum('erf,efd->erd', hidden_act, down_halves[:, half])))
        expert_out = (half_outs[0] + half_outs[1]).astype(jnp.bfloat16)
        picked = from_experts(expert_out, slots)
        layer_out = (values + lax.optimization_barrier(jnp.sum(weights[..., None] * picked, axis=2))).astype(jnp.bfloat16)
        outs_fwd.append(layer_out.reshape(TOKENS, D))
        values, inverse, normed = normalize(bwd_input[section_index].reshape(blocks, TOK_DEV, D), gain_row)
        slots = jax.vmap(slot_positions)(bwd_routes[section_index].reshape(blocks, TOK_DEV, TOPK))
        weights = bwd_gates[section_index].reshape(blocks, TOK_DEV, TOPK).astype(jnp.float32) / fixed_scale
        cotangent = bwd_cotangent[section_index].reshape(blocks, TOK_DEV, D).astype(jnp.float32)
        route_cot = (jnp.repeat(cotangent, TOPK, axis=1) * weights.reshape(blocks, TOK_DEV * TOPK, 1)).astype(jnp.bfloat16)
        rows_in = to_experts(jnp.repeat(normed, TOPK, axis=1), slots).astype(jnp.float32)
        rows_cot = to_experts(route_cot, slots).astype(jnp.float32)
        half_grads = []
        for half in range(2):
            gate_act = jnp.einsum('erd,edf->erf', rows_in, gate_halves[:, half])
            up_act = jnp.einsum('erd,edf->erf', rows_in, up_halves[:, half])
            sigma = jax.nn.sigmoid(gate_act)
            silu_val = gate_act * sigma
            act_grad = jnp.einsum('erd,efd->erf', rows_cot, down_halves[:, half])
            up_pre = rounded(act_grad * silu_val)
            gate_pre = rounded(act_grad * up_act * sigma * (1.0 + gate_act * (1.0 - sigma)))
            partial_value = jnp.einsum('erf,edf->erd', gate_pre, gate_halves[:, half]) + jnp.einsum('erf,edf->erd', up_pre, up_halves[:, half])
            half_grads.append(rounded(partial_value))
        route_grad = (half_grads[0] + half_grads[1]).astype(jnp.bfloat16)
        normed_grad = lax.optimization_barrier(jnp.sum(from_experts(route_grad, slots), axis=2))
        gains.append(lax.optimization_barrier(jnp.sum(normed_grad * values * inverse, axis=(0, 1))))
        scaled = normed_grad * gain_row
        inner_mean = lax.optimization_barrier(jnp.mean(scaled * values, axis=-1, keepdims=True))
        input_grad = inverse * (scaled - values * inverse * inverse * inner_mean)
        outs_bwd.append((cotangent + input_grad).astype(jnp.bfloat16).reshape(TOKENS, D))
    fwd_next = jnp.roll(jnp.stack(outs_fwd), 1, axis=0)
    bwd_next = jnp.roll(jnp.stack(outs_bwd), -1, axis=0)
    return (fwd_next, bwd_next, jnp.stack(gains))
```

```python
import functools
import jax
import jax.numpy as jnp
from jax import lax
from jax.experimental import pallas as pl
from jax.experimental.pallas import tpu as pltpu
from jax.sharding import PartitionSpec as P

EPS = 1e-06
GATE_SCALE = 1.0 / 65536.0
MESH = pl.DeviceIdType.MESH
F32 = jnp.float32
BF16 = jnp.bfloat16
CW = 512
HW = CW // 2
AHEAD = 4
FIRST = 7
NT = (((1,), (1,)), ((), ()))


def plane_offsets(ny, nx):
    offsets = [(dy, dx) for dy in range(ny) for dx in range(nx) if (dy, dx) != (0, 0)]

    def hops(o):
        return min(o[0], ny - o[0]) + min(o[1], nx - o[1])

    ranked = sorted(offsets, key=lambda o: (hops(o), (o[0] + o[1]) % 2, o))
    front, back = ranked[: len(ranked) // 2], ranked[len(ranked) // 2 :][::-1]
    mixed = []
    while front or back:
        if back:
            mixed.append(back.pop(0))
        if front:
            mixed.append(front.pop(0))
    return mixed


def pack(rows, blocks, cap):
    cube = rows.reshape(blocks, cap, CW)
    return jnp.concatenate([cube[:, :, :HW], cube[:, :, HW:]], axis=1).astype(BF16)


def unpack(cube, blocks, cap):
    return jnp.concatenate([cube[:, :cap], cube[:, cap:]], axis=2).reshape(blocks * cap, CW)


def body(
    sizes,
    fx_in, bx_in, ct_in, froute, fgate, broute, bgate, gain_in, wg_in, wu_in, wd_in,
    fnext, bnext, gain_out,
    fx, bx, ct, wg, wu, wd,
    normed, f_st, b_st, inv_b, wcol_f,
    dsend, drecv, xa, fsend, frecv, bsend, brecv,
    act_a, act_b, hid, su_b, gp_b, agrad, gpre, upre,
    ngrad, lout, tgrad, gsend, grecv, gsend2, grecv2,
    in_sem, w_ss, w_rs, d_ss, d_rs, f_ss, f_rs, b_ss, b_rs, sh_ss, sh_rs, g_ss, g_rs,
):
    ns, ny, nx, experts, cap, tok, width, hidden = sizes
    ne = ny * nx
    slots = experts * cap
    rows = ne * cap
    chunks = width // CW
    blk = 2 * cap
    half_d = width // 2
    half_h = hidden // 2
    wrow = half_d // chunks
    s, e, d = lax.axis_index("section"), lax.axis_index("expert"), lax.axis_index("dp")
    y, x = e // nx, lax.rem(e, nx)
    offsets = plane_offsets(ny, nx)
    plane = [lax.rem(y + dy, ny) * nx + lax.rem(x + dx, nx) for dy, dx in offsets]
    replica = (s, e, 1 - d)
    after = (lax.rem(s + 1, ns), e, d)
    before = (lax.rem(s + ns - 1, ns), e, d)

    barrier = pltpu.get_barrier_semaphore()
    for dev in [(s, t, d) for t in plane] + [replica, after, before]:
        pl.semaphore_signal(barrier, inc=1, device_id=dev, device_id_type=MESH)

    own = [
        pltpu.make_async_copy(fx_in, fx, in_sem.at[0]),
        pltpu.make_async_copy(bx_in, bx, in_sem.at[1]),
        pltpu.make_async_copy(ct_in, ct, in_sem.at[2]),
        pltpu.make_async_copy(wg_in, wg.at[pl.ds(pl.multiple_of(d * half_d, half_d), half_d)], in_sem.at[3]),
        pltpu.make_async_copy(wu_in, wu.at[pl.ds(pl.multiple_of(d * half_d, half_d), half_d)], in_sem.at[4]),
        pltpu.make_async_copy(wd_in, wd.at[pl.ds(pl.multiple_of(d * half_h, half_h), half_h)], in_sem.at[5]),
    ]
    for copy in own:
        copy.start()
    pl.semaphore_wait(barrier, len(plane) + 3)

    def weight_copy(j):
        if j < 2 * chunks:
            src, dst = (wg_in, wg) if j < chunks else (wu_in, wu)
            k = j % chunks
            src = src.at[pl.ds(k * wrow, wrow)]
            dst = dst.at[pl.ds(pl.multiple_of(d * half_d + k * wrow, wrow), wrow)]
        else:
            return down_copy(j - 2 * chunks)
        return pltpu.make_async_remote_copy(
            src_ref=src, dst_ref=dst, send_sem=w_ss.at[j], recv_sem=w_rs.at[j],
            device_id=replica, device_id_type=MESH,
        )

    def down_copy(c):
        cols = pl.ds(c * CW if isinstance(c, int) else pl.multiple_of(c * CW, CW), CW)
        return pltpu.make_async_remote_copy(
            src_ref=wd_in.at[:, cols],
            dst_ref=wd.at[pl.ds(pl.multiple_of(d * half_h, half_h), half_h), cols],
            send_sem=w_ss.at[2 * chunks + c], recv_sem=w_rs.at[2 * chunks + c],
            device_id=replica, device_id_type=MESH,
        )

    for j in range(FIRST):
        weight_copy(j).start()

    tok_r = lax.broadcasted_iota(jnp.int32, (tok, tok), 0)
    tok_c = lax.broadcasted_iota(jnp.int32, (tok, tok), 1)

    def column(row_ref):
        spread = jnp.broadcast_to(row_ref[...].astype(F32), (tok, tok))
        return jnp.sum(jnp.where(tok_r == tok_c, spread, 0.0), axis=1, keepdims=True)

    def slot_matrix(route_ref):
        route = column(route_ref)
        onehot = (route == tok_c.astype(F32)).astype(F32)
        below = (tok_c < tok_r).astype(F32).astype(BF16)
        earlier = jnp.dot(below, onehot.astype(BF16), preferred_element_type=F32)
        rank = jnp.sum(earlier * onehot, axis=1, keepdims=True)
        slot = route * float(cap) + rank
        lanes = lax.broadcasted_iota(jnp.int32, (tok, 2 * tok), 1).astype(F32)
        return (slot == lanes).astype(F32)

    step = 16

    def normalize(src, keep):
        @pl.loop(0, tok // step)
        def _(i):
            r = pl.ds(pl.multiple_of(i * step, step), step)
            v = src[r, :].astype(F32)
            inverse = lax.rsqrt(jnp.mean(v * v, axis=-1, keepdims=True) + EPS)
            if keep:
                inv_b[r, :] = jnp.broadcast_to(inverse, (step, 128))
            normed[r, :] = (v * inverse * gain_in[...]).astype(BF16)

    def dispatch(item, source, spread):
        @pl.loop(0, chunks)
        def _(c):
            cols = pl.ds(pl.multiple_of(c * CW, CW), CW)
            put = jnp.dot(spread, source[:, cols], preferred_element_type=F32)[:slots]
            dsend[item, :, pl.ds(pl.multiple_of(c * blk, blk), blk), :] = pack(put, experts, cap)

        for i, t in enumerate(plane):
            pltpu.make_async_remote_copy(
                src_ref=dsend.at[item, t // 2], dst_ref=drecv.at[item, e],
                send_sem=d_ss.at[item], recv_sem=d_rs.at[item],
                device_id=(s, t, d), device_id_type=MESH,
            ).start()
        pltpu.make_async_copy(dsend.at[item, e // 2], drecv.at[item, e], d_rs.at[item]).start()

    st = slot_matrix(froute)
    f_st[...] = st.astype(BF16)
    f_s = st.T.astype(BF16)
    wcol_f[...] = jnp.broadcast_to(column(fgate) * GATE_SCALE, (tok, 128))
    own[0].wait()
    normalize(fx, False)
    dispatch(0, normed, f_s)

    st = slot_matrix(broute)
    b_st[...] = st.astype(BF16)
    b_s = st.T.astype(BF16)
    own[1].wait()
    normalize(bx, True)
    dispatch(1, normed, b_s)

    own[2].wait()
    wcol_b = column(bgate) * GATE_SCALE

    normed[...] = (ct[...].astype(F32) * wcol_b).astype(BF16)
    dispatch(2, normed, b_s)

    for copy in own[3:]:
        copy.wait()

    def wait_weights(lo, hi):
        for j in range(lo, hi):
            weight_copy(j).wait_recv()
            if FIRST <= j + AHEAD < 3 * chunks:
                weight_copy(j + AHEAD).start()

    def arrived(item):
        pltpu.make_async_copy(drecv.at[item], drecv.at[item], d_rs.at[item]).wait()

    def received(item, c):
        cube = drecv[item, :, pl.ds(pl.multiple_of(c * blk, blk), blk), :]
        return unpack(cube.astype(F32), ne, cap).astype(BF16)

    def project(item, weight, total):
        total[...] = jnp.zeros_like(total)

        @pl.loop(0, chunks)
        def _(c):
            cols = pl.ds(pl.multiple_of(c * CW, CW), CW)
            total[...] += jnp.dot(xa[item, :, cols], weight[cols, :], preferred_element_type=F32)

    def relayout(item):
        arrived(item)

        @pl.loop(0, chunks)
        def _(c):
            xa[item, :, pl.ds(pl.multiple_of(c * CW, CW), CW)] = received(item, c)

    wait_weights(0, FIRST)
    relayout(0)
    relayout(1)
    project(0, wg, act_a)
    project(1, wg, su_b)
    wait_weights(FIRST, 2 * chunks)
    project(0, wu, act_b)
    a = act_a[...]
    hid[...] = (a * jax.nn.sigmoid(a) * act_b[...]).astype(BF16)
    project(1, wu, gp_b)
    a = su_b[...]
    sg = jax.nn.sigmoid(a)
    gp_b[...] = gp_b[...] * sg * (1.0 + a * (1.0 - sg))
    su_b[...] = a * sg
    agrad[...] = jnp.zeros_like(agrad)
    relayout(2)

    def give_back(send, recv, c, send_sem, recv_sem):
        part = pl.ds(pl.multiple_of(c * blk, blk), blk)
        for t in plane:
            pltpu.make_async_remote_copy(
                src_ref=send.at[t, part], dst_ref=recv.at[e, part],
                send_sem=send_sem, recv_sem=recv_sem,
                device_id=(s, t, d), device_id_type=MESH,
            ).start()
        pltpu.make_async_copy(send.at[e, part], recv.at[e, part], recv_sem).start()

    @pl.loop(0, chunks)
    def _(c):
        cols = pl.ds(pl.multiple_of(c * CW, CW), CW)
        down_copy(c).wait_recv()

        @pl.when(c + AHEAD < chunks)
        def _():
            down_copy(c + AHEAD).start()

        out = jnp.dot(hid[...], wd[:, cols], preferred_element_type=F32)
        fsend[:, pl.ds(pl.multiple_of(c * blk, blk), blk), :] = pack(out, ne, cap)
        give_back(fsend, frecv, c, f_ss, f_rs)
        agrad[...] += lax.dot_general(xa[2, :, cols], wd[:, cols], NT, preferred_element_type=F32)

    g = agrad[...]
    upre[...] = (g * su_b[...]).astype(BF16)
    gpre[...] = (g * gp_b[...]).astype(BF16)

    @pl.loop(0, chunks)
    def _(c):
        cols = pl.ds(pl.multiple_of(c * CW, CW), CW)
        grad = lax.dot_general(gpre[...], wg[cols, :], NT, preferred_element_type=F32)
        grad = grad + lax.dot_general(upre[...], wu[cols, :], NT, preferred_element_type=F32)
        bsend[:, pl.ds(pl.multiple_of(c * blk, blk), blk), :] = pack(grad, ne, cap)
        give_back(bsend, brecv, c, b_ss, b_rs.at[c])

    def picked(recv, c, gather):
        cube = recv[:, pl.ds(pl.multiple_of(c * blk, blk), blk), :].astype(F32)
        cube = cube.reshape(experts, 2, blk, HW)
        both = (cube[:, 0] + cube[:, 1]).astype(BF16).astype(F32)
        rows_in = unpack(both, experts, cap).astype(BF16)
        return jnp.dot(gather[:, :slots], rows_in, preferred_element_type=F32)

    pltpu.make_async_copy(frecv, frecv, f_rs).wait()

    @pl.loop(0, chunks)
    def _(c):
        cols = pl.ds(pl.multiple_of(c * CW, CW), CW)
        mixed = wcol_f[:, :1] * picked(frecv, c, f_st)
        lout[:, cols] = (fx[:, cols].astype(F32) + mixed).astype(BF16)

    f_shift = pltpu.make_async_remote_copy(
        src_ref=lout, dst_ref=fnext, send_sem=sh_ss.at[0], recv_sem=sh_rs.at[0],
        device_id=after, device_id_type=MESH,
    )
    f_shift.start()

    gsend[...] = jnp.zeros_like(gsend)

    def take(c, inner):
        cols = pl.ds(pl.multiple_of(c * CW, CW), CW)
        part = pl.ds(pl.multiple_of(c * blk, blk), blk)
        pltpu.make_async_copy(brecv.at[:, part], brecv.at[:, part], b_rs.at[c]).wait()
        ng = picked(brecv, c, b_st)
        v = bx[:, cols].astype(F32)
        gsend[pl.ds(c, 1), :] = jnp.sum(ng * v * inv_b[:, :1], axis=0, keepdims=True)
        scaled = ng * gain_in[:, cols]
        ngrad[:, cols] = scaled
        return inner + jnp.sum(scaled * v, axis=1, keepdims=True)

    inner = lax.fori_loop(0, chunks, take, jnp.zeros((tok, 1), F32))
    inverse = inv_b[:, :1]
    slope = inverse * inverse * (inner / float(width))

    for i, t in enumerate(plane):
        pltpu.make_async_remote_copy(
            src_ref=gsend, dst_ref=grecv.at[e], send_sem=g_ss.at[0], recv_sem=g_rs.at[0],
            device_id=(s, t, d), device_id_type=MESH,
        ).start()
    pltpu.make_async_copy(gsend, grecv.at[e], g_rs.at[0]).start()

    @pl.loop(0, chunks)
    def _(c):
        cols = pl.ds(pl.multiple_of(c * CW, CW), CW)
        grad = inverse * (ngrad[:, cols] - bx[:, cols].astype(F32) * slope)
        tgrad[:, cols] = (ct[:, cols].astype(F32) + grad).astype(BF16)

    b_shift = pltpu.make_async_remote_copy(
        src_ref=tgrad, dst_ref=bnext, send_sem=sh_ss.at[1], recv_sem=sh_rs.at[1],
        device_id=before, device_id_type=MESH,
    )
    b_shift.start()

    pltpu.make_async_copy(grecv, grecv, g_rs.at[0]).wait()
    gsend2[...] = jnp.sum(grecv[...], axis=0)
    across = pltpu.make_async_remote_copy(
        src_ref=gsend2, dst_ref=grecv2, send_sem=g_ss.at[1], recv_sem=g_rs.at[1],
        device_id=replica, device_id_type=MESH,
    )
    across.start()
    across.wait()
    gain_out[...] = gsend2[...] + grecv2[...]

    for j in range(3 * chunks):
        weight_copy(j).wait_send()
    others = ne - 1
    for item in range(3):
        pltpu.make_async_copy(
            drecv.at[item, pl.ds(0, others)], drecv.at[item, pl.ds(0, others)], d_ss.at[item]
        ).wait()
    for buf, sem in ((fsend, f_ss), (bsend, b_ss)):
        pltpu.make_async_copy(buf.at[pl.ds(0, others)], buf.at[pl.ds(0, others)], sem).wait()
    pltpu.make_async_copy(grecv.at[pl.ds(0, others)], grecv.at[pl.ds(0, others)], g_ss.at[0]).wait()
    f_shift.wait()
    b_shift.wait()


def on_device(
    sizes,
    fwd_input, fwd_routes, fwd_gates, bwd_input, bwd_cotangent, bwd_routes, bwd_gates,
    norm_gain, w_gate, w_up, w_down,
):
    ns, ny, nx, experts, cap, tok, width, hidden = sizes
    ne = ny * nx
    rows = ne * cap
    chunks = width // CW
    blk = 2 * cap
    anywhere = pl.BlockSpec(memory_space=pl.ANY)
    vmem = pl.BlockSpec(memory_space=pltpu.VMEM)
    sem = pltpu.SemaphoreType.DMA
    scratch = [
        pltpu.VMEM((tok, width), BF16),
        pltpu.VMEM((tok, width), BF16),
        pltpu.VMEM((tok, width), BF16),
        pltpu.VMEM((width, hidden), BF16),
        pltpu.VMEM((width, hidden), BF16),
        pltpu.VMEM((hidden, width), BF16),
        pltpu.VMEM((tok, width), BF16),
        pltpu.VMEM((tok, 2 * tok), BF16),
        pltpu.VMEM((tok, 2 * tok), BF16),
        pltpu.VMEM((tok, 128), F32),
        pltpu.VMEM((tok, 128), F32),
        pltpu.VMEM((3, experts, chunks * blk, HW), BF16),
        pltpu.VMEM((3, ne, chunks * blk, HW), BF16),
        pltpu.VMEM((3, rows, width), BF16),
        pltpu.VMEM((ne, chunks * blk, HW), BF16),
        pltpu.VMEM((ne, chunks * blk, HW), BF16),
        pltpu.VMEM((ne, chunks * blk, HW), BF16),
        pltpu.VMEM((ne, chunks * blk, HW), BF16),
        pltpu.VMEM((rows, hidden), F32),
        pltpu.VMEM((rows, hidden), F32),
        pltpu.VMEM((rows, hidden), BF16),
        pltpu.VMEM((rows, hidden), F32),
        pltpu.VMEM((rows, hidden), F32),
        pltpu.VMEM((rows, hidden), F32),
        pltpu.VMEM((rows, hidden), BF16),
        pltpu.VMEM((rows, hidden), BF16),
        pltpu.VMEM((tok, width), F32),
        pltpu.VMEM((tok, width), BF16),
        pltpu.VMEM((tok, width), BF16),
        pltpu.VMEM((8, CW), F32),
        pltpu.VMEM((ne, 8, CW), F32),
        pltpu.VMEM((8, CW), F32),
        pltpu.VMEM((8, CW), F32),
        sem((6,)),
        sem((3 * chunks,)),
        sem((3 * chunks,)),
        sem((3,)),
        sem((3,)),
        sem,
        sem,
        sem,
        sem((chunks,)),
        sem((2,)),
        sem((2,)),
        sem((2,)),
        sem((2,)),
    ]
    fnext, bnext, gain = pl.pallas_call(
        functools.partial(body, sizes),
        out_shape=[
            jax.ShapeDtypeStruct((tok, width), BF16),
            jax.ShapeDtypeStruct((tok, width), BF16),
            jax.ShapeDtypeStruct((8, CW), F32),
        ],
        in_specs=[anywhere] * 3 + [vmem] * 5 + [anywhere] * 3,
        out_specs=[anywhere, anywhere, vmem],
        scratch_shapes=scratch,
        compiler_params=pltpu.CompilerParams(
            collective_id=0, has_side_effects=True, vmem_limit_bytes=62 * 2**20
        ),
    )(
        fwd_input[0], bwd_input[0], bwd_cotangent[0],
        fwd_routes.reshape(1, tok), fwd_gates.reshape(1, tok),
        bwd_routes.reshape(1, tok), bwd_gates.reshape(1, tok),
        norm_gain, w_gate[0, 0], w_up[0, 0], w_down[0, 0],
    )
    return fnext[None], bnext[None], gain[:chunks].reshape(1, width)


def solution(mesh):
    ns, ne, ndp = mesh.shape["section"], mesh.shape["expert"], mesh.shape["dp"]
    ny = 4 if ne == 16 else 2
    sizes = (ns, ny, ne // ny, ne // 2, 24, 128, 3584, 512)
    tokens = P("section", ("expert", "dp"), None)
    return jax.shard_map(
        functools.partial(on_device, sizes),
        mesh=mesh,
        in_specs=(tokens,) * 7
        + (P("section", None),)
        + (P("section", "expert", "dp", None),) * 3,
        out_specs=(tokens, tokens, P("section", None)),
        check_vma=False,
    )
```

```python
import functools
import jax
import jax.numpy as jnp
from jax import lax
from jax.experimental import pallas as pl
from jax.experimental.pallas import tpu as pltpu
from jax.sharding import PartitionSpec as P

EPS = 1e-06
GATE_SCALE = 1.0 / 65536.0
MESH = pl.DeviceIdType.MESH
F32 = jnp.float32
BF16 = jnp.bfloat16
CW = 512
HW = CW // 2
AHEAD = 4
FIRST = 7
NT = (((1,), (1,)), ((), ()))


def plane_offsets(ny, nx):
    offsets = [(dy, dx) for dy in range(ny) for dx in range(nx) if (dy, dx) != (0, 0)]

    def hops(o):
        return min(o[0], ny - o[0]) + min(o[1], nx - o[1])

    ranked = sorted(offsets, key=lambda o: (hops(o), (o[0] + o[1]) % 2, o))
    front, back = ranked[: len(ranked) // 2], ranked[len(ranked) // 2 :][::-1]
    mixed = []
    while front or back:
        if back:
            mixed.append(back.pop(0))
        if front:
            mixed.append(front.pop(0))
    return mixed


def pack(rows, blocks, cap):
    cube = rows.reshape(blocks, cap, CW)
    return jnp.concatenate([cube[:, :, :HW], cube[:, :, HW:]], axis=1).astype(BF16)


def unpack(cube, blocks, cap):
    return jnp.concatenate([cube[:, :cap], cube[:, cap:]], axis=2).reshape(blocks * cap, CW)


def body(
    sizes,
    fx_in, bx_in, ct_in, froute, fgate, broute, bgate, gain_in, wg_in, wu_in, wd_in,
    fnext, bnext, gain_out,
    fx, bx, ct, wg, wu, wd,
    normed, f_st, b_st, b_oe, b_rk, inv_b, wcol_f,
    dsend, drecv, xa, fsend, frecv, bsend, brecv,
    act_a, act_b, hid, su_b, gp_b, agrad, gpre, upre,
    lout, tgrad, isend, irecv, gsend, grecv, gsend2, grecv2,
    in_sem, w_ss, w_rs, d_ss, d_rs, f_ss, f_rs, b_ss, b_rs, sh_ss, sh_rs, t_ss, t_rs, i_ss, i_rs, g_ss, g_rs,
):
    ns, ny, nx, experts, cap, tok, width, hidden = sizes
    ne = ny * nx
    slots = experts * cap
    rows = ne * cap
    chunks = width // CW
    blk = 2 * cap
    half_d = width // 2
    half_h = hidden // 2
    wrow = half_d // chunks
    s, e, d = lax.axis_index("section"), lax.axis_index("expert"), lax.axis_index("dp")
    y, x = e // nx, lax.rem(e, nx)
    offsets = plane_offsets(ny, nx)
    plane = [lax.rem(y + dy, ny) * nx + lax.rem(x + dx, nx) for dy, dx in offsets]
    replica = (s, e, 1 - d)
    after = (lax.rem(s + 1, ns), e, d)
    before = (lax.rem(s + ns - 1, ns), e, d)

    barrier = pltpu.get_barrier_semaphore()
    for dev in [(s, t, d) for t in plane] + [replica, after, before]:
        pl.semaphore_signal(barrier, inc=1, device_id=dev, device_id_type=MESH)

    own = [
        pltpu.make_async_copy(fx_in, fx, in_sem.at[0]),
        pltpu.make_async_copy(bx_in, bx, in_sem.at[1]),
        pltpu.make_async_copy(ct_in, ct, in_sem.at[2]),
        pltpu.make_async_copy(wg_in, wg.at[pl.ds(pl.multiple_of(d * half_d, half_d), half_d)], in_sem.at[3]),
        pltpu.make_async_copy(wu_in, wu.at[pl.ds(pl.multiple_of(d * half_d, half_d), half_d)], in_sem.at[4]),
        pltpu.make_async_copy(wd_in, wd.at[pl.ds(pl.multiple_of(d * half_h, half_h), half_h)], in_sem.at[5]),
    ]
    for copy in own:
        copy.start()
    pl.semaphore_wait(barrier, len(plane) + 3)

    def weight_copy(j):
        if j < 2 * chunks:
            src, dst = (wg_in, wg) if j < chunks else (wu_in, wu)
            k = j % chunks
            src = src.at[pl.ds(k * wrow, wrow)]
            dst = dst.at[pl.ds(pl.multiple_of(d * half_d + k * wrow, wrow), wrow)]
        else:
            return down_copy(j - 2 * chunks)
        return pltpu.make_async_remote_copy(
            src_ref=src, dst_ref=dst, send_sem=w_ss.at[j], recv_sem=w_rs.at[j],
            device_id=replica, device_id_type=MESH,
        )

    def down_copy(c):
        cols = pl.ds(c * CW if isinstance(c, int) else pl.multiple_of(c * CW, CW), CW)
        return pltpu.make_async_remote_copy(
            src_ref=wd_in.at[:, cols],
            dst_ref=wd.at[pl.ds(pl.multiple_of(d * half_h, half_h), half_h), cols],
            send_sem=w_ss.at[2 * chunks + c], recv_sem=w_rs.at[2 * chunks + c],
            device_id=replica, device_id_type=MESH,
        )

    for j in range(FIRST):
        weight_copy(j).start()

    tok_r = lax.broadcasted_iota(jnp.int32, (tok, tok), 0)
    tok_c = lax.broadcasted_iota(jnp.int32, (tok, tok), 1)

    def column(row_ref):
        spread = jnp.broadcast_to(row_ref[...].astype(F32), (tok, tok))
        return jnp.sum(jnp.where(tok_r == tok_c, spread, 0.0), axis=1, keepdims=True)

    def slot_matrix(route_ref):
        route = column(route_ref)
        onehot = (route == tok_c.astype(F32)).astype(F32)
        below = (tok_c < tok_r).astype(F32).astype(BF16)
        earlier = jnp.dot(below, onehot.astype(BF16), preferred_element_type=F32)
        rank = jnp.sum(earlier * onehot, axis=1, keepdims=True)
        slot = route * float(cap) + rank
        lanes = lax.broadcasted_iota(jnp.int32, (tok, 2 * tok), 1).astype(F32)
        return (slot == lanes).astype(F32), onehot, (rank == tok_c.astype(F32)).astype(F32)

    step = 16

    def normalize(src, keep):
        @pl.loop(0, tok // step)
        def _(i):
            r = pl.ds(pl.multiple_of(i * step, step), step)
            v = src[r, :].astype(F32)
            inverse = lax.rsqrt(jnp.mean(v * v, axis=-1, keepdims=True) + EPS)
            if keep:
                inv_b[r, :] = jnp.broadcast_to(inverse, (step, 128))
            normed[r, :] = (v * inverse * gain_in[...]).astype(BF16)

    def dispatch(item, source, spread):
        @pl.loop(0, chunks)
        def _(c):
            cols = pl.ds(pl.multiple_of(c * CW, CW), CW)
            put = jnp.dot(spread, source[:, cols], preferred_element_type=F32)[:slots]
            dsend[item, :, pl.ds(pl.multiple_of(c * blk, blk), blk), :] = pack(put, experts, cap)

        for i, t in enumerate(plane):
            pltpu.make_async_remote_copy(
                src_ref=dsend.at[item, t // 2], dst_ref=drecv.at[item, e],
                send_sem=d_ss.at[item], recv_sem=d_rs.at[item],
                device_id=(s, t, d), device_id_type=MESH,
            ).start()
        pltpu.make_async_copy(dsend.at[item, e // 2], drecv.at[item, e], d_rs.at[item]).start()

    st, _, _ = slot_matrix(froute)
    f_st[...] = st.astype(BF16)
    f_s = st.T.astype(BF16)
    wcol_f[...] = jnp.broadcast_to(column(fgate) * GATE_SCALE, (tok, 128))
    own[0].wait()
    normalize(fx, False)
    dispatch(0, normed, f_s)

    st, b_oe[...], b_rk[...] = slot_matrix(broute)
    b_st[...] = st.astype(BF16)
    b_s = st.T.astype(BF16)
    own[1].wait()
    normalize(bx, True)
    dispatch(1, normed, b_s)

    own[2].wait()
    wcol_b = column(bgate) * GATE_SCALE

    normed[...] = (ct[...].astype(F32) * wcol_b).astype(BF16)
    dispatch(2, normed, b_s)

    for copy in own[3:]:
        copy.wait()

    def wait_weights(lo, hi):
        for j in range(lo, hi):
            weight_copy(j).wait_recv()
            if FIRST <= j + AHEAD < 3 * chunks:
                weight_copy(j + AHEAD).start()

    def arrived(item):
        pltpu.make_async_copy(drecv.at[item], drecv.at[item], d_rs.at[item]).wait()

    def received(item, c):
        cube = drecv[item, :, pl.ds(pl.multiple_of(c * blk, blk), blk), :]
        return unpack(cube.astype(F32), ne, cap).astype(BF16)

    def project(item, weight, total):
        total[...] = jnp.zeros_like(total)

        @pl.loop(0, chunks)
        def _(c):
            cols = pl.ds(pl.multiple_of(c * CW, CW), CW)
            total[...] += jnp.dot(xa[item, :, cols], weight[cols, :], preferred_element_type=F32)

    def relayout(item):
        arrived(item)

        @pl.loop(0, chunks)
        def _(c):
            xa[item, :, pl.ds(pl.multiple_of(c * CW, CW), CW)] = received(item, c)

    wait_weights(0, FIRST)
    relayout(0)
    relayout(1)
    project(0, wg, act_a)
    project(1, wg, su_b)
    wait_weights(FIRST, 2 * chunks)
    project(0, wu, act_b)
    a = act_a[...]
    hid[...] = (a * jax.nn.sigmoid(a) * act_b[...]).astype(BF16)
    project(1, wu, gp_b)
    a = su_b[...]
    sg = jax.nn.sigmoid(a)
    b = gp_b[...]
    gp = b * sg * (1.0 + a * (1.0 - sg))
    gp_b[...] = gp
    su_b[...] = a * sg
    act_a[...] = a * gp + b * (a * sg)
    agrad[...] = jnp.zeros_like(agrad)
    relayout(2)

    def give_back(send, recv, c, send_sem, recv_sem):
        part = pl.ds(pl.multiple_of(c * blk, blk), blk)
        for t in plane:
            pltpu.make_async_remote_copy(
                src_ref=send.at[t, part], dst_ref=recv.at[e, part],
                send_sem=send_sem, recv_sem=recv_sem,
                device_id=(s, t, d), device_id_type=MESH,
            ).start()
        pltpu.make_async_copy(send.at[e, part], recv.at[e, part], recv_sem).start()

    def forward_chunk(c):
        cols = pl.ds(c * CW if isinstance(c, int) else pl.multiple_of(c * CW, CW), CW)
        out = jnp.dot(hid[...], wd[:, cols], preferred_element_type=F32)
        part = pl.ds(c * blk if isinstance(c, int) else pl.multiple_of(c * blk, blk), blk)
        fsend[:, part, :] = pack(out, ne, cap)
        give_back(fsend, frecv, c, f_ss, f_rs)

    @pl.loop(0, chunks)
    def _(c):
        cols = pl.ds(pl.multiple_of(c * CW, CW), CW)
        down_copy(c).wait_recv()

        @pl.when(c + AHEAD < chunks)
        def _():
            down_copy(c + AHEAD).start()

        agrad[...] += lax.dot_general(xa[2, :, cols], wd[:, cols], NT, preferred_element_type=F32)

        @pl.when(c < chunks - 1)
        def _():
            forward_chunk(c)

    g = agrad[...]
    upre[...] = (g * su_b[...]).astype(BF16)
    gpre[...] = (g * gp_b[...]).astype(BF16)

    dots = jnp.sum(g * act_a[...], axis=1, keepdims=True)
    dots = jnp.broadcast_to(dots, (rows, 128)).reshape(ne, cap, 128)
    place = lax.broadcasted_iota(jnp.int32, (ne, cap, 128), 1)
    lane = lax.broadcasted_iota(jnp.int32, (ne, cap, 128), 2)
    dots = jnp.sum(jnp.where(place == lane, dots, 0.0), axis=1, keepdims=True)
    isend[...] = jnp.broadcast_to(dots, (ne, 8, 128))
    for t in plane:
        pltpu.make_async_remote_copy(
            src_ref=isend.at[t], dst_ref=irecv.at[e], send_sem=i_ss, recv_sem=i_rs,
            device_id=(s, t, d), device_id_type=MESH,
        ).start()
    pltpu.make_async_copy(isend.at[e], irecv.at[e], i_rs).start()
    gsend[...] = jnp.zeros_like(gsend)

    @pl.loop(0, chunks)
    def _(c):
        cols = pl.ds(pl.multiple_of(c * CW, CW), CW)
        grad = lax.dot_general(gpre[...], wg[cols, :], NT, preferred_element_type=F32)
        grad = grad + lax.dot_general(upre[...], wu[cols, :], NT, preferred_element_type=F32)
        bsend[:, pl.ds(pl.multiple_of(c * blk, blk), blk), :] = pack(grad, ne, cap)
        give_back(bsend, brecv, c, b_ss, b_rs.at[c])
        total = jnp.sum(grad * xa[1, :, cols].astype(F32), axis=0, keepdims=True)
        gsend[pl.ds(c, 1), :] = total / gain_in[:, cols]

        @pl.when(c == 0)
        def _():
            forward_chunk(chunks - 1)

    for t in plane:
        pltpu.make_async_remote_copy(
            src_ref=gsend, dst_ref=grecv.at[e], send_sem=g_ss.at[0], recv_sem=g_rs.at[0],
            device_id=(s, t, d), device_id_type=MESH,
        ).start()
    pltpu.make_async_copy(gsend, grecv.at[e], g_rs.at[0]).start()

    def picked(recv, c, gather):
        cube = recv[:, pl.ds(pl.multiple_of(c * blk, blk), blk), :].astype(F32)
        cube = cube.reshape(experts, 2, blk, HW)
        both = (cube[:, 0] + cube[:, 1]).astype(BF16).astype(F32)
        rows_in = unpack(both, experts, cap).astype(BF16)
        return jnp.dot(gather[:, :slots], rows_in, preferred_element_type=F32)

    pltpu.make_async_copy(frecv, frecv, f_rs).wait()

    @pl.loop(0, chunks)
    def _(c):
        cols = pl.ds(pl.multiple_of(c * CW, CW), CW)
        mixed = wcol_f[:, :1] * picked(frecv, c, f_st)
        lout[:, cols] = (fx[:, cols].astype(F32) + mixed).astype(BF16)

    f_shift = pltpu.make_async_remote_copy(
        src_ref=lout, dst_ref=fnext, send_sem=sh_ss, recv_sem=sh_rs,
        device_id=after, device_id_type=MESH,
    )
    f_shift.start()

    pltpu.make_async_copy(irecv, irecv, i_rs).wait()
    per_expert = jnp.sum(irecv[...].reshape(experts, 2, 8, 128), axis=1)
    spread = jnp.zeros((tok, 128), F32)
    for k in range(experts):
        spread = spread + b_oe[:, k : k + 1] * per_expert[k, :1, :]
    inverse = inv_b[:, :1]
    slope = inverse * jnp.sum(spread * b_rk[...], axis=1, keepdims=True) * (1.0 / width)
    inv_b[...] = jnp.broadcast_to(inverse, (tok, 128))
    b_rk[...] = jnp.broadcast_to(inverse * slope, (tok, 128))

    def shift_chunk(c):
        cols = pl.ds(c * CW if isinstance(c, int) else pl.multiple_of(c * CW, CW), CW)
        return pltpu.make_async_remote_copy(
            src_ref=tgrad.at[:, cols], dst_ref=bnext.at[:, cols],
            send_sem=t_ss.at[c], recv_sem=t_rs.at[c],
            device_id=before, device_id_type=MESH,
        )

    def take(c):
        cols = pl.ds(pl.multiple_of(c * CW, CW), CW)
        part = pl.ds(pl.multiple_of(c * blk, blk), blk)
        pltpu.make_async_copy(brecv.at[:, part], brecv.at[:, part], b_rs.at[c]).wait()
        scaled = picked(brecv, c, b_st) * gain_in[:, cols]
        grad = inv_b[:, :1] * scaled - bx[:, cols].astype(F32) * b_rk[:, :1]
        tgrad[:, cols] = (ct[:, cols].astype(F32) + grad).astype(BF16)
        shift_chunk(c).start()

    pl.loop(0, chunks - 1)(take)

    pltpu.make_async_copy(grecv, grecv, g_rs.at[0]).wait()
    gsend2[...] = jnp.sum(grecv[...], axis=0)
    across = pltpu.make_async_remote_copy(
        src_ref=gsend2, dst_ref=grecv2, send_sem=g_ss.at[1], recv_sem=g_rs.at[1],
        device_id=replica, device_id_type=MESH,
    )
    across.start()
    take(chunks - 1)
    across.wait()
    for c in range(chunks):
        gain_out[:, c * CW : (c + 1) * CW] = gsend2[c : c + 1, :] + grecv2[c : c + 1, :]

    for j in range(3 * chunks):
        weight_copy(j).wait_send()
    others = ne - 1
    for item in range(3):
        pltpu.make_async_copy(
            drecv.at[item, pl.ds(0, others)], drecv.at[item, pl.ds(0, others)], d_ss.at[item]
        ).wait()
    for buf, sem in ((fsend, f_ss), (bsend, b_ss)):
        pltpu.make_async_copy(buf.at[pl.ds(0, others)], buf.at[pl.ds(0, others)], sem).wait()
    pltpu.make_async_copy(grecv.at[pl.ds(0, others)], grecv.at[pl.ds(0, others)], g_ss.at[0]).wait()
    pltpu.make_async_copy(isend.at[pl.ds(0, others)], isend.at[pl.ds(0, others)], i_ss).wait()
    f_shift.wait()
    for c in range(chunks):
        shift_chunk(c).wait()


def on_device(
    sizes,
    fwd_input, fwd_routes, fwd_gates, bwd_input, bwd_cotangent, bwd_routes, bwd_gates,
    norm_gain, w_gate, w_up, w_down,
):
    ns, ny, nx, experts, cap, tok, width, hidden = sizes
    ne = ny * nx
    rows = ne * cap
    chunks = width // CW
    blk = 2 * cap
    anywhere = pl.BlockSpec(memory_space=pl.ANY)
    vmem = pl.BlockSpec(memory_space=pltpu.VMEM)
    sem = pltpu.SemaphoreType.DMA
    scratch = [
        pltpu.VMEM((tok, width), BF16),
        pltpu.VMEM((tok, width), BF16),
        pltpu.VMEM((tok, width), BF16),
        pltpu.VMEM((width, hidden), BF16),
        pltpu.VMEM((width, hidden), BF16),
        pltpu.VMEM((hidden, width), BF16),
        pltpu.VMEM((tok, width), BF16),
        pltpu.VMEM((tok, 2 * tok), BF16),
        pltpu.VMEM((tok, 2 * tok), BF16),
        pltpu.VMEM((tok, 128), F32),
        pltpu.VMEM((tok, 128), F32),
        pltpu.VMEM((tok, 128), F32),
        pltpu.VMEM((tok, 128), F32),
        pltpu.VMEM((3, experts, chunks * blk, HW), BF16),
        pltpu.VMEM((3, ne, chunks * blk, HW), BF16),
        pltpu.VMEM((3, rows, width), BF16),
        pltpu.VMEM((ne, chunks * blk, HW), BF16),
        pltpu.VMEM((ne, chunks * blk, HW), BF16),
        pltpu.VMEM((ne, chunks * blk, HW), BF16),
        pltpu.VMEM((ne, chunks * blk, HW), BF16),
        pltpu.VMEM((rows, hidden), F32),
        pltpu.VMEM((rows, hidden), F32),
        pltpu.VMEM((rows, hidden), BF16),
        pltpu.VMEM((rows, hidden), F32),
        pltpu.VMEM((rows, hidden), F32),
        pltpu.VMEM((rows, hidden), F32),
        pltpu.VMEM((rows, hidden), BF16),
        pltpu.VMEM((rows, hidden), BF16),
        pltpu.VMEM((tok, width), BF16),
        pltpu.VMEM((tok, width), BF16),
        pltpu.VMEM((ne, 8, 128), F32),
        pltpu.VMEM((ne, 8, 128), F32),
        pltpu.VMEM((8, CW), F32),
        pltpu.VMEM((ne, 8, CW), F32),
        pltpu.VMEM((8, CW), F32),
        pltpu.VMEM((8, CW), F32),
        sem((6,)),
        sem((3 * chunks,)),
        sem((3 * chunks,)),
        sem((3,)),
        sem((3,)),
        sem,
        sem,
        sem,
        sem((chunks,)),
        sem,
        sem,
        sem((chunks,)),
        sem((chunks,)),
        sem,
        sem,
        sem((2,)),
        sem((2,)),
    ]
    fnext, bnext, gain = pl.pallas_call(
        functools.partial(body, sizes),
        out_shape=[
            jax.ShapeDtypeStruct((tok, width), BF16),
            jax.ShapeDtypeStruct((tok, width), BF16),
            jax.ShapeDtypeStruct((1, width), F32),
        ],
        in_specs=[anywhere] * 3 + [vmem] * 5 + [anywhere] * 3,
        out_specs=[anywhere, anywhere, vmem],
        scratch_shapes=scratch,
        compiler_params=pltpu.CompilerParams(
            collective_id=0, has_side_effects=True, vmem_limit_bytes=62 * 2**20
        ),
    )(
        fwd_input[0], bwd_input[0], bwd_cotangent[0],
        fwd_routes.reshape(1, tok), fwd_gates.reshape(1, tok),
        bwd_routes.reshape(1, tok), bwd_gates.reshape(1, tok),
        norm_gain, w_gate[0, 0], w_up[0, 0], w_down[0, 0],
    )
    return fnext[None], bnext[None], gain


def solution(mesh):
    ns, ne, ndp = mesh.shape["section"], mesh.shape["expert"], mesh.shape["dp"]
    ny = 4 if ne == 16 else 2
    sizes = (ns, ny, ne // ny, ne // 2, 24, 128, 3584, 512)
    tokens = P("section", ("expert", "dp"), None)
    return jax.shard_map(
        functools.partial(on_device, sizes),
        mesh=mesh,
        in_specs=(tokens,) * 7
        + (P("section", None),)
        + (P("section", "expert", "dp", None),) * 3,
        out_specs=(tokens, tokens, P("section", None)),
        check_vma=False,
    )
```

```python
import functools
import jax
import jax.numpy as jnp
from jax import lax
from jax.experimental import pallas as pl
from jax.experimental.pallas import tpu as pltpu
from jax.sharding import PartitionSpec as P

EPS = 1e-06
GATE_SCALE = 1.0 / 65536.0
MESH = pl.DeviceIdType.MESH
F32 = jnp.float32
BF16 = jnp.bfloat16
CW = 256
HW = CW // 2
AHEAD = 14
FIRST = 28
NT = (((1,), (1,)), ((), ()))


def plane_offsets(ny, nx):
    offsets = [(dy, dx) for dy in range(ny) for dx in range(nx) if (dy, dx) != (0, 0)]

    def hops(o):
        return min(o[0], ny - o[0]) + min(o[1], nx - o[1])

    ranked = sorted(offsets, key=lambda o: (hops(o), (o[0] + o[1]) % 2, o))
    front, back = ranked[: len(ranked) // 2], ranked[len(ranked) // 2 :][::-1]
    mixed = []
    while front or back:
        if back:
            mixed.append(back.pop(0))
        if front:
            mixed.append(front.pop(0))
    return mixed


def pack(rows, blocks, cap):
    cube = rows.reshape(blocks, cap, CW)
    return jnp.concatenate([cube[:, :, :HW], cube[:, :, HW:]], axis=1).astype(BF16)


def unpack(cube, blocks, cap):
    return jnp.concatenate([cube[:, :cap], cube[:, cap:]], axis=2).reshape(blocks * cap, CW)


def body(
    sizes,
    fx_in, bx_in, ct_in, froute, fgate, broute, bgate, gain_in, wg_in, wu_in, wd_in,
    fnext, bnext, gain_out,
    fx, bx, ct, wg, wu, wd,
    normed, f_st, b_st, b_oe, b_rk, inv_b, wcol_f,
    dsend, drecv, xa, fsend, frecv, bsend, brecv,
    act_a, act_b, hid, su_b, gp_b, agrad, gpre, upre,
    lout, tgrad, isend, irecv, gsend, gsend2, grecv, grecv2,
    in_sem, w_ss, w_rs, d_ss, d_rs, f_ss, f_rs, b_ss, b_rs, sh_ss, sh_rs, t_ss, t_rs, i_ss, i_rs, g_ss, g_rs,
):
    ns, ny, nx, experts, cap, tok, width, hidden = sizes
    ne = ny * nx
    slots = experts * cap
    rows = ne * cap
    chunks = width // CW
    blk = 2 * cap
    half_d = width // 2
    half_h = hidden // 2
    wrow = half_d // chunks
    s, e, d = lax.axis_index("section"), lax.axis_index("expert"), lax.axis_index("dp")
    y, x = e // nx, lax.rem(e, nx)
    offsets = plane_offsets(ny, nx)
    plane = [lax.rem(y + dy, ny) * nx + lax.rem(x + dx, nx) for dy, dx in offsets]
    replica = (s, e, 1 - d)
    after = (lax.rem(s + 1, ns), e, d)
    before = (lax.rem(s + ns - 1, ns), e, d)

    barrier = pltpu.get_barrier_semaphore()
    for dev in [(s, t, d) for t in plane] + [replica, after, before]:
        pl.semaphore_signal(barrier, inc=1, device_id=dev, device_id_type=MESH)

    own = [
        pltpu.make_async_copy(fx_in, fx, in_sem.at[0]),
        pltpu.make_async_copy(bx_in, bx, in_sem.at[1]),
        pltpu.make_async_copy(ct_in, ct, in_sem.at[2]),
        pltpu.make_async_copy(wg_in, wg.at[pl.ds(pl.multiple_of(d * half_d, half_d), half_d)], in_sem.at[3]),
        pltpu.make_async_copy(wu_in, wu.at[pl.ds(pl.multiple_of(d * half_d, half_d), half_d)], in_sem.at[4]),
    ]
    own_rows = pl.ds(pl.multiple_of(d * half_h, half_h), half_h)
    for c in range(chunks):
        pltpu.make_async_copy(
            wd_in.at[:, pl.ds(c * CW, CW)], wd.at[c, own_rows], in_sem.at[5]
        ).start()
    for copy in own:
        copy.start()
    pl.semaphore_wait(barrier, len(plane) + 3)

    def weight_copy(j):
        if j < 2 * chunks:
            src, dst = (wg_in, wg) if j < chunks else (wu_in, wu)
            k = j % chunks
            src = src.at[pl.ds(k * wrow, wrow)]
            dst = dst.at[pl.ds(pl.multiple_of(d * half_d + k * wrow, wrow), wrow)]
        else:
            return down_copy(j - 2 * chunks)
        return pltpu.make_async_remote_copy(
            src_ref=src, dst_ref=dst, send_sem=w_ss.at[j], recv_sem=w_rs.at[j],
            device_id=replica, device_id_type=MESH,
        )

    def down_copy(c):
        return pltpu.make_async_remote_copy(
            src_ref=wd.at[c, own_rows],
            dst_ref=wd.at[c, own_rows],
            send_sem=w_ss.at[2 * chunks + c], recv_sem=w_rs.at[2 * chunks + c],
            device_id=replica, device_id_type=MESH,
        )

    for j in range(FIRST):
        weight_copy(j).start()

    tok_r = lax.broadcasted_iota(jnp.int32, (tok, tok), 0)
    tok_c = lax.broadcasted_iota(jnp.int32, (tok, tok), 1)

    def column(row_ref):
        spread = jnp.broadcast_to(row_ref[...].astype(F32), (tok, tok))
        return jnp.sum(jnp.where(tok_r == tok_c, spread, 0.0), axis=1, keepdims=True)

    def slot_matrix(route_ref):
        route = column(route_ref)
        onehot = (route == tok_c.astype(F32)).astype(F32)
        below = (tok_c < tok_r).astype(F32).astype(BF16)
        earlier = jnp.dot(below, onehot.astype(BF16), preferred_element_type=F32)
        rank = jnp.sum(earlier * onehot, axis=1, keepdims=True)
        slot = route * float(cap) + rank
        lanes = lax.broadcasted_iota(jnp.int32, (tok, 2 * tok), 1).astype(F32)
        return (slot == lanes).astype(F32), onehot, (rank == tok_c.astype(F32)).astype(F32)

    step = 16

    def normalize(src, keep):
        @pl.loop(0, tok // step)
        def _(i):
            r = pl.ds(pl.multiple_of(i * step, step), step)
            v = src[r, :].astype(F32)
            inverse = lax.rsqrt(jnp.mean(v * v, axis=-1, keepdims=True) + EPS)
            if keep:
                inv_b[r, :] = jnp.broadcast_to(inverse, (step, 128))
            normed[r, :] = (v * inverse * gain_in[...]).astype(BF16)

    def dispatch(item, source, spread):
        @pl.loop(0, chunks)
        def _(c):
            cols = pl.ds(pl.multiple_of(c * CW, CW), CW)
            put = jnp.dot(spread, source[:, cols], preferred_element_type=F32)[:slots]
            dsend[item, :, pl.ds(pl.multiple_of(c * blk, blk), blk), :] = pack(put, experts, cap)

        for i, t in enumerate(plane):
            pltpu.make_async_remote_copy(
                src_ref=dsend.at[item, t // 2], dst_ref=drecv.at[item, e],
                send_sem=d_ss.at[item], recv_sem=d_rs.at[item],
                device_id=(s, t, d), device_id_type=MESH,
            ).start()
        pltpu.make_async_copy(dsend.at[item, e // 2], drecv.at[item, e], d_rs.at[item]).start()

    st, _, _ = slot_matrix(froute)
    f_st[...] = st.astype(BF16)
    f_s = st.T.astype(BF16)
    wcol_f[...] = jnp.broadcast_to(column(fgate) * GATE_SCALE, (tok, 128))
    own[0].wait()
    normalize(fx, False)
    dispatch(0, normed, f_s)

    st, b_oe[...], b_rk[...] = slot_matrix(broute)
    b_st[...] = st.astype(BF16)
    b_s = st.T.astype(BF16)
    own[1].wait()
    normalize(bx, True)
    dispatch(1, normed, b_s)

    own[2].wait()
    wcol_b = column(bgate) * GATE_SCALE

    normed[...] = (ct[...].astype(F32) * wcol_b).astype(BF16)
    dispatch(2, normed, b_s)

    for copy in own[3:]:
        copy.wait()
    pltpu.make_async_copy(wd.at[:, own_rows], wd.at[:, own_rows], in_sem.at[5]).wait()

    def wait_weights(lo, hi):
        for j in range(lo, hi):
            weight_copy(j).wait_recv()
            if FIRST <= j + AHEAD < 3 * chunks:
                weight_copy(j + AHEAD).start()

    def arrived(item):
        pltpu.make_async_copy(drecv.at[item], drecv.at[item], d_rs.at[item]).wait()

    def received(item, c):
        cube = drecv[item, :, pl.ds(pl.multiple_of(c * blk, blk), blk), :]
        return unpack(cube.astype(F32), ne, cap).astype(BF16)

    def project(item, weight, total):
        total[...] = jnp.zeros_like(total)

        @pl.loop(0, chunks)
        def _(c):
            cols = pl.ds(pl.multiple_of(c * CW, CW), CW)
            total[...] += jnp.dot(xa[item, :, cols], weight[cols, :], preferred_element_type=F32)

    def relayout(item):
        arrived(item)

        @pl.loop(0, chunks)
        def _(c):
            xa[item, :, pl.ds(pl.multiple_of(c * CW, CW), CW)] = received(item, c)

    wait_weights(0, chunks)
    relayout(0)
    relayout(1)
    project(0, wg, act_a)
    project(1, wg, su_b)
    wait_weights(chunks, 2 * chunks)
    project(0, wu, act_b)
    a = act_a[...]
    hid[...] = (a * jax.nn.sigmoid(a) * act_b[...]).astype(BF16)
    project(1, wu, gp_b)
    a = su_b[...]
    sg = jax.nn.sigmoid(a)
    b = gp_b[...]
    gp = b * sg * (1.0 + a * (1.0 - sg))
    gp_b[...] = gp
    su_b[...] = a * sg
    act_a[...] = a * gp + b * (a * sg)
    agrad[...] = jnp.zeros_like(agrad)
    relayout(2)

    def give_back(send, recv, c, send_sem, recv_sem):
        part = pl.ds(pl.multiple_of(c * blk, blk), blk)
        for t in plane:
            pltpu.make_async_remote_copy(
                src_ref=send.at[t, part], dst_ref=recv.at[e, part],
                send_sem=send_sem, recv_sem=recv_sem,
                device_id=(s, t, d), device_id_type=MESH,
            ).start()
        pltpu.make_async_copy(send.at[e, part], recv.at[e, part], recv_sem).start()

    def forward_chunk(c):
        out = jnp.dot(hid[...], wd[c], preferred_element_type=F32)
        part = pl.ds(c * blk if isinstance(c, int) else pl.multiple_of(c * blk, blk), blk)
        fsend[:, part, :] = pack(out, ne, cap)
        give_back(fsend, frecv, c, f_ss, f_rs)

    @pl.loop(0, chunks)
    def _(c):
        cols = pl.ds(pl.multiple_of(c * CW, CW), CW)
        down_copy(c).wait_recv()

        @pl.when(c + AHEAD < chunks)
        def _():
            down_copy(c + AHEAD).start()

        agrad[...] += lax.dot_general(xa[2, :, cols], wd[c], NT, preferred_element_type=F32)

        @pl.when(c < chunks - 1)
        def _():
            forward_chunk(c)

    g = agrad[...]
    upre[...] = (g * su_b[...]).astype(BF16)
    gpre[...] = (g * gp_b[...]).astype(BF16)

    dots = jnp.sum(g * act_a[...], axis=1, keepdims=True)
    dots = jnp.broadcast_to(dots, (rows, 128)).reshape(ne, cap, 128)
    place = lax.broadcasted_iota(jnp.int32, (ne, cap, 128), 1)
    lane = lax.broadcasted_iota(jnp.int32, (ne, cap, 128), 2)
    dots = jnp.sum(jnp.where(place == lane, dots, 0.0), axis=1, keepdims=True)
    isend[...] = jnp.broadcast_to(dots, (ne, 8, 128))
    for t in plane:
        pltpu.make_async_remote_copy(
            src_ref=isend.at[t], dst_ref=irecv.at[e], send_sem=i_ss, recv_sem=i_rs,
            device_id=(s, t, d), device_id_type=MESH,
        ).start()
    pltpu.make_async_copy(isend.at[e], irecv.at[e], i_rs).start()
    gsend[...] = jnp.zeros_like(gsend)

    def backward_chunk(c):
        cols = pl.ds(pl.multiple_of(c * CW, CW), CW)
        grad = lax.dot_general(gpre[...], wg[cols, :], NT, preferred_element_type=F32)
        grad = grad + lax.dot_general(upre[...], wu[cols, :], NT, preferred_element_type=F32)
        bsend[:, pl.ds(pl.multiple_of(c * blk, blk), blk), :] = pack(grad, ne, cap)
        total = jnp.sum(grad * xa[1, :, cols].astype(F32), axis=0, keepdims=True)
        gsend[pl.ds(c, 1), :] = total / gain_in[:, cols]

    def backward_send(c):
        give_back(bsend, brecv, c, b_ss, b_rs.at[c])

    held = chunks * 9 // 14

    @pl.loop(0, held)
    def _(c):
        backward_chunk(c)
        backward_send(c)

        @pl.when(c == 1)
        def _():
            forward_chunk(chunks - 1)

    pl.loop(held, chunks)(backward_chunk)
    for t in plane:
        pltpu.make_async_remote_copy(
            src_ref=gsend, dst_ref=grecv.at[e], send_sem=g_ss.at[0], recv_sem=g_rs.at[0],
            device_id=(s, t, d), device_id_type=MESH,
        ).start()
    pltpu.make_async_copy(gsend, grecv.at[e], g_rs.at[0]).start()
    pl.loop(held, chunks)(backward_send)

    def picked(recv, c, gather):
        cube = recv[:, pl.ds(pl.multiple_of(c * blk, blk), blk), :].astype(F32)
        cube = cube.reshape(experts, 2, blk, HW)
        both = (cube[:, 0] + cube[:, 1]).astype(BF16).astype(F32)
        rows_in = unpack(both, experts, cap).astype(BF16)
        return jnp.dot(gather[:, :slots], rows_in, preferred_element_type=F32)

    pltpu.make_async_copy(frecv, frecv, f_rs).wait()

    @pl.loop(0, chunks)
    def _(c):
        cols = pl.ds(pl.multiple_of(c * CW, CW), CW)
        mixed = wcol_f[:, :1] * picked(frecv, c, f_st)
        lout[:, cols] = (fx[:, cols].astype(F32) + mixed).astype(BF16)

    f_shift = pltpu.make_async_remote_copy(
        src_ref=lout, dst_ref=fnext, send_sem=sh_ss, recv_sem=sh_rs,
        device_id=after, device_id_type=MESH,
    )
    f_shift.start()

    pltpu.make_async_copy(irecv, irecv, i_rs).wait()
    per_expert = jnp.sum(irecv[...].reshape(experts, 2, 8, 128), axis=1)
    spread = jnp.zeros((tok, 128), F32)
    for k in range(experts):
        spread = spread + b_oe[:, k : k + 1] * per_expert[k, :1, :]
    inverse = inv_b[:, :1]
    slope = inverse * jnp.sum(spread * b_rk[...], axis=1, keepdims=True) * (1.0 / width)
    inv_b[...] = jnp.broadcast_to(inverse, (tok, 128))
    b_rk[...] = jnp.broadcast_to(inverse * slope, (tok, 128))

    def shift_chunk(c):
        cols = pl.ds(c * CW if isinstance(c, int) else pl.multiple_of(c * CW, CW), CW)
        return pltpu.make_async_remote_copy(
            src_ref=tgrad.at[:, cols], dst_ref=bnext.at[:, cols],
            send_sem=t_ss.at[c], recv_sem=t_rs.at[c],
            device_id=before, device_id_type=MESH,
        )

    def take(c):
        cols = pl.ds(pl.multiple_of(c * CW, CW), CW)
        part = pl.ds(pl.multiple_of(c * blk, blk), blk)
        pltpu.make_async_copy(brecv.at[:, part], brecv.at[:, part], b_rs.at[c]).wait()
        scaled = picked(brecv, c, b_st) * gain_in[:, cols]
        grad = inv_b[:, :1] * scaled - bx[:, cols].astype(F32) * b_rk[:, :1]
        tgrad[:, cols] = (ct[:, cols].astype(F32) + grad).astype(BF16)
        shift_chunk(c).start()

    pl.loop(0, held)(take)

    pltpu.make_async_copy(grecv, grecv, g_rs.at[0]).wait()
    gsend2[...] = jnp.sum(grecv[...], axis=0)
    across = pltpu.make_async_remote_copy(
        src_ref=gsend2, dst_ref=grecv2, send_sem=g_ss.at[1], recv_sem=g_rs.at[1],
        device_id=replica, device_id_type=MESH,
    )
    across.start()
    pl.loop(held, chunks)(take)
    across.wait()
    for c in range(chunks):
        gain_out[:, c * CW : (c + 1) * CW] = gsend2[c : c + 1, :] + grecv2[c : c + 1, :]

    for j in range(3 * chunks):
        weight_copy(j).wait_send()
    others = ne - 1
    for item in range(3):
        pltpu.make_async_copy(
            drecv.at[item, pl.ds(0, others)], drecv.at[item, pl.ds(0, others)], d_ss.at[item]
        ).wait()
    for buf, sem in ((fsend, f_ss), (bsend, b_ss)):
        pltpu.make_async_copy(buf.at[pl.ds(0, others)], buf.at[pl.ds(0, others)], sem).wait()
    pltpu.make_async_copy(grecv.at[pl.ds(0, others)], grecv.at[pl.ds(0, others)], g_ss.at[0]).wait()
    pltpu.make_async_copy(isend.at[pl.ds(0, others)], isend.at[pl.ds(0, others)], i_ss).wait()
    f_shift.wait()
    for c in range(chunks):
        shift_chunk(c).wait()


def on_device(
    sizes,
    fwd_input, fwd_routes, fwd_gates, bwd_input, bwd_cotangent, bwd_routes, bwd_gates,
    norm_gain, w_gate, w_up, w_down,
):
    ns, ny, nx, experts, cap, tok, width, hidden = sizes
    ne = ny * nx
    rows = ne * cap
    chunks = width // CW
    blk = 2 * cap
    anywhere = pl.BlockSpec(memory_space=pl.ANY)
    vmem = pl.BlockSpec(memory_space=pltpu.VMEM)
    sem = pltpu.SemaphoreType.DMA
    scratch = [
        pltpu.VMEM((tok, width), BF16),
        pltpu.VMEM((tok, width), BF16),
        pltpu.VMEM((tok, width), BF16),
        pltpu.VMEM((width, hidden), BF16),
        pltpu.VMEM((width, hidden), BF16),
        pltpu.VMEM((chunks, hidden, CW), BF16),
        pltpu.VMEM((tok, width), BF16),
        pltpu.VMEM((tok, 2 * tok), BF16),
        pltpu.VMEM((tok, 2 * tok), BF16),
        pltpu.VMEM((tok, 128), F32),
        pltpu.VMEM((tok, 128), F32),
        pltpu.VMEM((tok, 128), F32),
        pltpu.VMEM((tok, 128), F32),
        pltpu.VMEM((3, experts, chunks * blk, HW), BF16),
        pltpu.VMEM((3, ne, chunks * blk, HW), BF16),
        pltpu.VMEM((3, rows, width), BF16),
        pltpu.VMEM((ne, chunks * blk, HW), BF16),
        pltpu.VMEM((ne, chunks * blk, HW), BF16),
        pltpu.VMEM((ne, chunks * blk, HW), BF16),
        pltpu.VMEM((ne, chunks * blk, HW), BF16),
        pltpu.VMEM((rows, hidden), F32),
        pltpu.VMEM((rows, hidden), F32),
        pltpu.VMEM((rows, hidden), BF16),
        pltpu.VMEM((rows, hidden), F32),
        pltpu.VMEM((rows, hidden), F32),
        pltpu.VMEM((rows, hidden), F32),
        pltpu.VMEM((rows, hidden), BF16),
        pltpu.VMEM((rows, hidden), BF16),
        pltpu.VMEM((tok, width), BF16),
        pltpu.VMEM((tok, width), BF16),
        pltpu.VMEM((ne, 8, 128), F32),
        pltpu.VMEM((ne, 8, 128), F32),
        pltpu.VMEM((16, CW), F32),
        pltpu.VMEM((16, CW), F32),
        pltpu.VMEM((ne, 16, CW), F32),
        pltpu.VMEM((16, CW), F32),
        sem((6,)),
        sem((3 * chunks,)),
        sem((3 * chunks,)),
        sem((3,)),
        sem((3,)),
        sem,
        sem,
        sem,
        sem((chunks,)),
        sem,
        sem,
        sem((chunks,)),
        sem((chunks,)),
        sem,
        sem,
        sem((2,)),
        sem((2,)),
    ]
    fnext, bnext, gain = pl.pallas_call(
        functools.partial(body, sizes),
        out_shape=[
            jax.ShapeDtypeStruct((tok, width), BF16),
            jax.ShapeDtypeStruct((tok, width), BF16),
            jax.ShapeDtypeStruct((1, width), F32),
        ],
        in_specs=[anywhere] * 3 + [vmem] * 5 + [anywhere] * 3,
        out_specs=[anywhere, anywhere, vmem],
        scratch_shapes=scratch,
        compiler_params=pltpu.CompilerParams(
            collective_id=0, has_side_effects=True, vmem_limit_bytes=62 * 2**20
        ),
    )(
        fwd_input[0], bwd_input[0], bwd_cotangent[0],
        fwd_routes.reshape(1, tok), fwd_gates.reshape(1, tok),
        bwd_routes.reshape(1, tok), bwd_gates.reshape(1, tok),
        norm_gain, w_gate[0, 0], w_up[0, 0], w_down[0, 0],
    )
    return fnext[None], bnext[None], gain


def solution(mesh):
    ns, ne, ndp = mesh.shape["section"], mesh.shape["expert"], mesh.shape["dp"]
    ny = 4 if ne == 16 else 2
    sizes = (ns, ny, ne // ny, ne // 2, 24, 128, 3584, 512)
    tokens = P("section", ("expert", "dp"), None)
    return jax.shard_map(
        functools.partial(on_device, sizes),
        mesh=mesh,
        in_specs=(tokens,) * 7
        + (P("section", None),)
        + (P("section", "expert", "dp", None),) * 3,
        out_specs=(tokens, tokens, P("section", None)),
        check_vma=False,
    )
```

```python
import functools
import jax
import jax.numpy as jnp
from jax import lax
from jax.experimental import pallas as pl
from jax.experimental.pallas import tpu as pltpu
from jax.sharding import PartitionSpec as P

EPS = 1e-06
GATE_SCALE = 1.0 / 65536.0
MESH = pl.DeviceIdType.MESH
F32 = jnp.float32
BF16 = jnp.bfloat16
CW = 256
HW = CW // 2
AHEAD = 14
FIRST = 28
LAG = 4
NT = (((1,), (1,)), ((), ()))


def plane_offsets(ny, nx):
    offsets = [(dy, dx) for dy in range(ny) for dx in range(nx) if (dy, dx) != (0, 0)]

    def hops(o):
        return min(o[0], ny - o[0]) + min(o[1], nx - o[1])

    ranked = sorted(offsets, key=lambda o: (hops(o), (o[0] + o[1]) % 2, o))
    front, back = ranked[: len(ranked) // 2], ranked[len(ranked) // 2 :][::-1]
    mixed = []
    while front or back:
        if back:
            mixed.append(back.pop(0))
        if front:
            mixed.append(front.pop(0))
    return mixed


def pack(rows, blocks, cap):
    cube = rows.reshape(blocks, cap, CW)
    return jnp.concatenate([cube[:, :, :HW], cube[:, :, HW:]], axis=1).astype(BF16)


def unpack(cube, blocks, cap):
    return jnp.concatenate([cube[:, :cap], cube[:, cap:]], axis=2).reshape(blocks * cap, CW)


def body(
    sizes,
    fx_in, bx_in, ct_in, froute, fgate, broute, bgate, gain_in, wg_in, wu_in, wd_in,
    fnext, bnext, gain_out,
    fx, bx, ct, wg, wu, wd,
    normed, f_st, b_st, b_oe, b_rk, inv_b, wcol_f,
    dsend, drecv, xa, fsend, frecv, bsend, brecv,
    act_a, act_b, hid, su_b, gp_b, agrad, gpre, upre,
    lout, tgrad, isend, irecv, gsend, gsend2, gsend3, grecv, grecv2,
    in_sem, w_ss, w_rs, d_ss, d_rs, f_ss, f_rs, b_ss, b_rs, sh_ss, sh_rs, t_ss, t_rs, i_ss, i_rs, g_ss, g_rs,
):
    ns, ny, nx, experts, cap, tok, width, hidden = sizes
    ne = ny * nx
    slots = experts * cap
    rows = ne * cap
    chunks = width // CW
    blk = 2 * cap
    half_d = width // 2
    half_h = hidden // 2
    wrow = half_d // chunks
    s, e, d = lax.axis_index("section"), lax.axis_index("expert"), lax.axis_index("dp")
    y, x = e // nx, lax.rem(e, nx)
    offsets = plane_offsets(ny, nx)
    plane = [lax.rem(y + dy, ny) * nx + lax.rem(x + dx, nx) for dy, dx in offsets]
    replica = (s, e, 1 - d)
    after = (lax.rem(s + 1, ns), e, d)
    before = (lax.rem(s + ns - 1, ns), e, d)

    barrier = pltpu.get_barrier_semaphore()
    for dev in [(s, t, d) for t in plane] + [replica, after, before]:
        pl.semaphore_signal(barrier, inc=1, device_id=dev, device_id_type=MESH)

    own = [
        pltpu.make_async_copy(fx_in, fx, in_sem.at[0]),
        pltpu.make_async_copy(bx_in, bx, in_sem.at[1]),
        pltpu.make_async_copy(ct_in, ct, in_sem.at[2]),
        pltpu.make_async_copy(wg_in, wg.at[pl.ds(pl.multiple_of(d * half_d, half_d), half_d)], in_sem.at[3]),
        pltpu.make_async_copy(wu_in, wu.at[pl.ds(pl.multiple_of(d * half_d, half_d), half_d)], in_sem.at[4]),
    ]
    own_rows = pl.ds(pl.multiple_of(d * half_h, half_h), half_h)
    for c in range(chunks):
        pltpu.make_async_copy(
            wd_in.at[:, pl.ds(c * CW, CW)], wd.at[c, own_rows], in_sem.at[5]
        ).start()
    for copy in own:
        copy.start()
    pl.semaphore_wait(barrier, len(plane) + 3)

    def weight_copy(j):
        if j < 2 * chunks:
            src, dst = (wg_in, wg) if j < chunks else (wu_in, wu)
            k = j % chunks
            src = src.at[pl.ds(k * wrow, wrow)]
            dst = dst.at[pl.ds(pl.multiple_of(d * half_d + k * wrow, wrow), wrow)]
        else:
            return down_copy(j - 2 * chunks)
        return pltpu.make_async_remote_copy(
            src_ref=src, dst_ref=dst, send_sem=w_ss.at[j], recv_sem=w_rs.at[j],
            device_id=replica, device_id_type=MESH,
        )

    def down_copy(c):
        return pltpu.make_async_remote_copy(
            src_ref=wd.at[c, own_rows],
            dst_ref=wd.at[c, own_rows],
            send_sem=w_ss.at[2 * chunks + c], recv_sem=w_rs.at[2 * chunks + c],
            device_id=replica, device_id_type=MESH,
        )

    for j in range(FIRST):
        weight_copy(j).start()

    tok_r = lax.broadcasted_iota(jnp.int32, (tok, tok), 0)
    tok_c = lax.broadcasted_iota(jnp.int32, (tok, tok), 1)

    def column(row_ref):
        spread = jnp.broadcast_to(row_ref[...].astype(F32), (tok, tok))
        return jnp.sum(jnp.where(tok_r == tok_c, spread, 0.0), axis=1, keepdims=True)

    def slot_matrix(route_ref):
        route = column(route_ref)
        onehot = (route == tok_c.astype(F32)).astype(F32)
        below = (tok_c < tok_r).astype(F32).astype(BF16)
        earlier = jnp.dot(below, onehot.astype(BF16), preferred_element_type=F32)
        rank = jnp.sum(earlier * onehot, axis=1, keepdims=True)
        slot = route * float(cap) + rank
        lanes = lax.broadcasted_iota(jnp.int32, (tok, 2 * tok), 1).astype(F32)
        return (slot == lanes).astype(F32), onehot, (rank == tok_c.astype(F32)).astype(F32)

    step = 16

    def normalize(src, keep):
        @pl.loop(0, tok // step)
        def _(i):
            r = pl.ds(pl.multiple_of(i * step, step), step)
            v = src[r, :].astype(F32)
            inverse = lax.rsqrt(jnp.mean(v * v, axis=-1, keepdims=True) + EPS)
            if keep:
                inv_b[r, :] = jnp.broadcast_to(inverse, (step, 128))
            normed[r, :] = (v * inverse * gain_in[...]).astype(BF16)

    def dispatch(item, source, spread):
        @pl.loop(0, chunks)
        def _(c):
            cols = pl.ds(pl.multiple_of(c * CW, CW), CW)
            put = jnp.dot(spread, source[:, cols], preferred_element_type=F32)[:slots]
            dsend[item, :, pl.ds(pl.multiple_of(c * blk, blk), blk), :] = pack(put, experts, cap)

        for i, t in enumerate(plane):
            pltpu.make_async_remote_copy(
                src_ref=dsend.at[item, t // 2], dst_ref=drecv.at[item, e],
                send_sem=d_ss.at[item], recv_sem=d_rs.at[item],
                device_id=(s, t, d), device_id_type=MESH,
            ).start()
        pltpu.make_async_copy(dsend.at[item, e // 2], drecv.at[item, e], d_rs.at[item]).start()

    st, _, _ = slot_matrix(froute)
    f_st[...] = st.astype(BF16)
    f_s = st.T.astype(BF16)
    wcol_f[...] = jnp.broadcast_to(column(fgate) * GATE_SCALE, (tok, 128))
    own[0].wait()
    normalize(fx, False)
    dispatch(0, normed, f_s)

    st, b_oe[...], b_rk[...] = slot_matrix(broute)
    b_st[...] = st.astype(BF16)
    b_s = st.T.astype(BF16)
    own[1].wait()
    normalize(bx, True)
    dispatch(1, normed, b_s)

    own[2].wait()
    wcol_b = column(bgate) * GATE_SCALE

    normed[...] = (ct[...].astype(F32) * wcol_b).astype(BF16)
    dispatch(2, normed, b_s)

    for copy in own[3:]:
        copy.wait()
    pltpu.make_async_copy(wd.at[:, own_rows], wd.at[:, own_rows], in_sem.at[5]).wait()

    def wait_weights(lo, hi):
        for j in range(lo, hi):
            weight_copy(j).wait_recv()
            if FIRST <= j + AHEAD < 3 * chunks:
                weight_copy(j + AHEAD).start()

    def arrived(item):
        pltpu.make_async_copy(drecv.at[item], drecv.at[item], d_rs.at[item]).wait()

    def received(item, c):
        cube = drecv[item, :, pl.ds(pl.multiple_of(c * blk, blk), blk), :]
        return unpack(cube.astype(F32), ne, cap).astype(BF16)

    def project(item, weight, total):
        total[...] = jnp.zeros_like(total)

        @pl.loop(0, chunks)
        def _(c):
            cols = pl.ds(pl.multiple_of(c * CW, CW), CW)
            total[...] += jnp.dot(xa[item, :, cols], weight[cols, :], preferred_element_type=F32)

    def relayout(item):
        arrived(item)

        @pl.loop(0, chunks)
        def _(c):
            xa[item, :, pl.ds(pl.multiple_of(c * CW, CW), CW)] = received(item, c)

    wait_weights(0, chunks)
    relayout(0)
    relayout(1)
    project(0, wg, act_a)
    project(1, wg, su_b)
    wait_weights(chunks, 2 * chunks)
    project(0, wu, act_b)
    a = act_a[...]
    hid[...] = (a * jax.nn.sigmoid(a) * act_b[...]).astype(BF16)
    project(1, wu, gp_b)
    a = su_b[...]
    sg = jax.nn.sigmoid(a)
    b = gp_b[...]
    gp = b * sg * (1.0 + a * (1.0 - sg))
    gp_b[...] = gp
    su_b[...] = a * sg
    act_a[...] = a * gp + b * (a * sg)
    agrad[...] = jnp.zeros_like(agrad)
    relayout(2)

    def give_back(send, recv, c, send_sem, recv_sem):
        part = pl.ds(c * blk if isinstance(c, int) else pl.multiple_of(c * blk, blk), blk)
        for t in plane:
            pltpu.make_async_remote_copy(
                src_ref=send.at[t, part], dst_ref=recv.at[e, part],
                send_sem=send_sem, recv_sem=recv_sem,
                device_id=(s, t, d), device_id_type=MESH,
            ).start()
        pltpu.make_async_copy(send.at[e, part], recv.at[e, part], recv_sem).start()

    def picked(recv, c, gather):
        cube = recv[:, pl.ds(pl.multiple_of(c * blk, blk), blk), :].astype(F32)
        cube = cube.reshape(experts, 2, blk, HW)
        both = (cube[:, 0] + cube[:, 1]).astype(BF16).astype(F32)
        rows_in = unpack(both, experts, cap).astype(BF16)
        return jnp.dot(gather[:, :slots], rows_in, preferred_element_type=F32)

    def forward_take(c):
        cols = pl.ds(pl.multiple_of(c * CW, CW), CW)
        part = pl.ds(pl.multiple_of(c * blk, blk), blk)
        pltpu.make_async_copy(frecv.at[:, part], frecv.at[:, part], f_rs.at[c]).wait()
        mixed = wcol_f[:, :1] * picked(frecv, c, f_st)
        lout[:, cols] = (fx[:, cols].astype(F32) + mixed).astype(BF16)

    split = (chunks - LAG) * CW
    f_shifts = [
        pltpu.make_async_remote_copy(
            src_ref=lout.at[:, pl.ds(start, size)], dst_ref=fnext.at[:, pl.ds(start, size)],
            send_sem=sh_ss.at[i], recv_sem=sh_rs.at[i],
            device_id=after, device_id_type=MESH,
        )
        for i, (start, size) in enumerate(((0, split), (split, width - split)))
    ]

    def forward_chunk(c):
        out = jnp.dot(hid[...], wd[c], preferred_element_type=F32)
        part = pl.ds(c * blk if isinstance(c, int) else pl.multiple_of(c * blk, blk), blk)
        fsend[:, part, :] = pack(out, ne, cap)
        give_back(fsend, frecv, c, f_ss, f_rs.at[c])

    @pl.loop(0, chunks)
    def _(c):
        cols = pl.ds(pl.multiple_of(c * CW, CW), CW)
        down_copy(c).wait_recv()

        @pl.when(c + AHEAD < chunks)
        def _():
            down_copy(c + AHEAD).start()

        agrad[...] += lax.dot_general(xa[2, :, cols], wd[c], NT, preferred_element_type=F32)

        @pl.when(c < chunks - 1)
        def _():
            forward_chunk(c)

        @pl.when(c >= LAG)
        def _():
            forward_take(c - LAG)

    f_shifts[0].start()
    g = agrad[...]
    upre[...] = (g * su_b[...]).astype(BF16)
    gpre[...] = (g * gp_b[...]).astype(BF16)

    gsend[...] = jnp.zeros_like(gsend)

    def backward_chunk(c):
        cols = pl.ds(c * CW if isinstance(c, int) else pl.multiple_of(c * CW, CW), CW)
        grad = lax.dot_general(gpre[...], wg[cols, :], NT, preferred_element_type=F32)
        grad = grad + lax.dot_general(upre[...], wu[cols, :], NT, preferred_element_type=F32)
        bsend[:, pl.ds(c * blk if isinstance(c, int) else pl.multiple_of(c * blk, blk), blk), :] = pack(grad, ne, cap)
        total = jnp.sum(grad * xa[1, :, cols].astype(F32), axis=0, keepdims=True)
        gsend[pl.ds(c, 1), :] = total / gain_in[:, cols]

    def backward_send(c):
        give_back(bsend, brecv, c, b_ss, b_rs.at[c])

    held = chunks * 9 // 14

    backward_chunk(0)
    backward_send(0)
    dots = jnp.sum(g * act_a[...], axis=1, keepdims=True)
    dots = jnp.broadcast_to(dots, (rows, 128)).reshape(ne, cap, 128)
    place = lax.broadcasted_iota(jnp.int32, (ne, cap, 128), 1)
    lane = lax.broadcasted_iota(jnp.int32, (ne, cap, 128), 2)
    dots = jnp.sum(jnp.where(place == lane, dots, 0.0), axis=1, keepdims=True)
    isend[...] = jnp.broadcast_to(dots, (ne, 8, 128))
    for t in plane:
        pltpu.make_async_remote_copy(
            src_ref=isend.at[t], dst_ref=irecv.at[e], send_sem=i_ss, recv_sem=i_rs,
            device_id=(s, t, d), device_id_type=MESH,
        ).start()
    pltpu.make_async_copy(isend.at[e], irecv.at[e], i_rs).start()
    forward_chunk(chunks - 1)

    @pl.loop(1, held)
    def _(c):
        backward_chunk(c)
        backward_send(c)

    pl.loop(held, chunks)(backward_chunk)
    def share(stage, src, index, others):
        for t in others:
            pltpu.make_async_remote_copy(
                src_ref=src, dst_ref=grecv.at[stage, index],
                send_sem=g_ss.at[stage], recv_sem=g_rs.at[stage],
                device_id=(s, t, d), device_id_type=MESH,
            ).start()
        pltpu.make_async_copy(src, grecv.at[stage, index], g_rs.at[stage]).start()

    def shared(stage):
        pltpu.make_async_copy(grecv.at[stage], grecv.at[stage], g_rs.at[stage]).wait()
        return jnp.sum(grecv[stage], axis=0)

    share(0, gsend, y, [lax.rem(y + k, ny) * nx + x for k in range(1, ny)])
    pl.loop(held, chunks)(backward_send)

    pl.loop(chunks - LAG, chunks)(forward_take)
    f_shifts[1].start()

    pltpu.make_async_copy(irecv, irecv, i_rs).wait()
    per_expert = jnp.sum(irecv[...].reshape(experts, 2, 8, 128), axis=1)
    spread = jnp.zeros((tok, 128), F32)
    for k in range(experts):
        spread = spread + b_oe[:, k : k + 1] * per_expert[k, :1, :]
    inverse = inv_b[:, :1]
    slope = inverse * jnp.sum(spread * b_rk[...], axis=1, keepdims=True) * (1.0 / width)
    inv_b[...] = jnp.broadcast_to(inverse, (tok, 128))
    b_rk[...] = jnp.broadcast_to(inverse * slope, (tok, 128))

    def shift_chunk(c):
        cols = pl.ds(c * CW if isinstance(c, int) else pl.multiple_of(c * CW, CW), CW)
        return pltpu.make_async_remote_copy(
            src_ref=tgrad.at[:, cols], dst_ref=bnext.at[:, cols],
            send_sem=t_ss.at[c], recv_sem=t_rs.at[c],
            device_id=before, device_id_type=MESH,
        )

    def take(c):
        cols = pl.ds(pl.multiple_of(c * CW, CW), CW)
        part = pl.ds(pl.multiple_of(c * blk, blk), blk)
        pltpu.make_async_copy(brecv.at[:, part], brecv.at[:, part], b_rs.at[c]).wait()
        scaled = picked(brecv, c, b_st) * gain_in[:, cols]
        grad = inv_b[:, :1] * scaled - bx[:, cols].astype(F32) * b_rk[:, :1]
        tgrad[:, cols] = (ct[:, cols].astype(F32) + grad).astype(BF16)
        shift_chunk(c).start()

    pl.loop(0, held // 2 + 1)(take)

    gsend2[...] = shared(0)
    share(1, gsend2, x, [y * nx + lax.rem(x + k, nx) for k in range(1, nx)])
    pl.loop(held // 2 + 1, held + 1)(take)
    gsend3[...] = shared(1)
    across = pltpu.make_async_remote_copy(
        src_ref=gsend3, dst_ref=grecv2, send_sem=g_ss.at[2], recv_sem=g_rs.at[2],
        device_id=replica, device_id_type=MESH,
    )
    across.start()
    pl.loop(held + 1, chunks)(take)
    across.wait()
    for c in range(chunks):
        gain_out[:, c * CW : (c + 1) * CW] = gsend3[c : c + 1, :] + grecv2[c : c + 1, :]

    for j in range(3 * chunks):
        weight_copy(j).wait_send()
    others = ne - 1
    for item in range(3):
        pltpu.make_async_copy(
            drecv.at[item, pl.ds(0, others)], drecv.at[item, pl.ds(0, others)], d_ss.at[item]
        ).wait()
    for buf, sem in ((fsend, f_ss), (bsend, b_ss)):
        pltpu.make_async_copy(buf.at[pl.ds(0, others)], buf.at[pl.ds(0, others)], sem).wait()
    for stage, count in ((0, ny - 1), (1, nx - 1)):
        sent = grecv.at[stage, pl.ds(0, count)]
        pltpu.make_async_copy(sent, sent, g_ss.at[stage]).wait()
    pltpu.make_async_copy(isend.at[pl.ds(0, others)], isend.at[pl.ds(0, others)], i_ss).wait()
    for shift in f_shifts:
        shift.wait()
    for c in range(chunks):
        shift_chunk(c).wait()


def on_device(
    sizes,
    fwd_input, fwd_routes, fwd_gates, bwd_input, bwd_cotangent, bwd_routes, bwd_gates,
    norm_gain, w_gate, w_up, w_down,
):
    ns, ny, nx, experts, cap, tok, width, hidden = sizes
    ne = ny * nx
    rows = ne * cap
    chunks = width // CW
    blk = 2 * cap
    anywhere = pl.BlockSpec(memory_space=pl.ANY)
    vmem = pl.BlockSpec(memory_space=pltpu.VMEM)
    sem = pltpu.SemaphoreType.DMA
    scratch = [
        pltpu.VMEM((tok, width), BF16),
        pltpu.VMEM((tok, width), BF16),
        pltpu.VMEM((tok, width), BF16),
        pltpu.VMEM((width, hidden), BF16),
        pltpu.VMEM((width, hidden), BF16),
        pltpu.VMEM((chunks, hidden, CW), BF16),
        pltpu.VMEM((tok, width), BF16),
        pltpu.VMEM((tok, 2 * tok), BF16),
        pltpu.VMEM((tok, 2 * tok), BF16),
        pltpu.VMEM((tok, 128), F32),
        pltpu.VMEM((tok, 128), F32),
        pltpu.VMEM((tok, 128), F32),
        pltpu.VMEM((tok, 128), F32),
        pltpu.VMEM((3, experts, chunks * blk, HW), BF16),
        pltpu.VMEM((3, ne, chunks * blk, HW), BF16),
        pltpu.VMEM((3, rows, width), BF16),
        pltpu.VMEM((ne, chunks * blk, HW), BF16),
        pltpu.VMEM((ne, chunks * blk, HW), BF16),
        pltpu.VMEM((ne, chunks * blk, HW), BF16),
        pltpu.VMEM((ne, chunks * blk, HW), BF16),
        pltpu.VMEM((rows, hidden), F32),
        pltpu.VMEM((rows, hidden), F32),
        pltpu.VMEM((rows, hidden), BF16),
        pltpu.VMEM((rows, hidden), F32),
        pltpu.VMEM((rows, hidden), F32),
        pltpu.VMEM((rows, hidden), F32),
        pltpu.VMEM((rows, hidden), BF16),
        pltpu.VMEM((rows, hidden), BF16),
        pltpu.VMEM((tok, width), BF16),
        pltpu.VMEM((tok, width), BF16),
        pltpu.VMEM((ne, 8, 128), F32),
        pltpu.VMEM((ne, 8, 128), F32),
        pltpu.VMEM((16, CW), F32),
        pltpu.VMEM((16, CW), F32),
        pltpu.VMEM((16, CW), F32),
        pltpu.VMEM((2, max(ny, nx), 16, CW), F32),
        pltpu.VMEM((16, CW), F32),
        sem((6,)),
        sem((3 * chunks,)),
        sem((3 * chunks,)),
        sem((3,)),
        sem((3,)),
        sem,
        sem((chunks,)),
        sem,
        sem((chunks,)),
        sem((2,)),
        sem((2,)),
        sem((chunks,)),
        sem((chunks,)),
        sem,
        sem,
        sem((3,)),
        sem((3,)),
    ]
    fnext, bnext, gain = pl.pallas_call(
        functools.partial(body, sizes),
        out_shape=[
            jax.ShapeDtypeStruct((tok, width), BF16),
            jax.ShapeDtypeStruct((tok, width), BF16),
            jax.ShapeDtypeStruct((1, width), F32),
        ],
        in_specs=[anywhere] * 3 + [vmem] * 5 + [anywhere] * 3,
        out_specs=[anywhere, anywhere, vmem],
        scratch_shapes=scratch,
        compiler_params=pltpu.CompilerParams(
            collective_id=0, has_side_effects=True, vmem_limit_bytes=62 * 2**20
        ),
    )(
        fwd_input[0], bwd_input[0], bwd_cotangent[0],
        fwd_routes.reshape(1, tok), fwd_gates.reshape(1, tok),
        bwd_routes.reshape(1, tok), bwd_gates.reshape(1, tok),
        norm_gain, w_gate[0, 0], w_up[0, 0], w_down[0, 0],
    )
    return fnext[None], bnext[None], gain


def solution(mesh):
    ns, ne, ndp = mesh.shape["section"], mesh.shape["expert"], mesh.shape["dp"]
    ny = 4 if ne == 16 else 2
    sizes = (ns, ny, ne // ny, ne // 2, 24, 128, 3584, 512)
    tokens = P("section", ("expert", "dp"), None)
    return jax.shard_map(
        functools.partial(on_device, sizes),
        mesh=mesh,
        in_specs=(tokens,) * 7
        + (P("section", None),)
        + (P("section", "expert", "dp", None),) * 3,
        out_specs=(tokens, tokens, P("section", None)),
        check_vma=False,
    )
```
